128 devices in a mesh: dp: 16 (over z_lo, y, core), inner: 8 (over x, z_hi).
Axes of the slice: x: 4, y: 4, z: 4 (z_hi: 2, z_lo: 2; z = z_hi * 2 + z_lo), core: 2. Of those that a mesh axis runs over, the one named last changes fastest.
Arguments:
- image_embed: bfloat16 [16384, 1152], P(('dp', 'inner')), may hold values from -6 to 6
- text_embed: bfloat16 [16384, 1152], P(('dp', 'inner')), may hold values from -6 to 6
- image_head: bfloat16 [1152, 1152], replicated, may hold values from -0.1875 to 0.1875
- text_head: bfloat16 [1152, 1152], replicated, may hold values from -0.1875 to 0.1875
- pair_ids: int32 [16384], P(('dp', 'inner')), may hold values from 0 to 4095, never falling along the last dimension, each value on 1 to 8 neighbouring positions
- logit_scale: float32 [1], replicated, may hold values from 8 to 24
- logit_bias: float32 [1], replicated, may hold values from -4 to -1.5
Outputs:
- grad_image_head: float32 [1152, 1152], replicated
- grad_text_head: float32 [1152, 1152], replicated
The draws below stay inside these ranges and needn't reach their ends.
Inputs may be any that keep to these rules, and one draw needn't show every extreme that they name: pair_ids never falls along the pairs; each id covers 1 to 8 consecutive pairs, and some id covers exactly 8.
All inputs are finite; a program needn't handle non-finite values.
Results may differ from the reference program's by a relative error of at most 0.0025.
Values may be sent and summed in bfloat16 or wider, within the bound.
No kernel may reach another device: no remote copies, remote signals or barrier semaphores. Data moves between devices by JAX's collectives and lax.ppermute only.
A program may use at most 128 MiB of HBM per device.

```python
import math
import jax
import jax.numpy as jnp
import numpy as np
from jax import lax

EMBED = 1152
PROJ = 1152
TOK_DEV = 128
TOKENS = 16384
N_INNER = 8


def steps_of(key, dims, split, low, top_value):
    level, own = 1.0, jax.random.fold_in(key, 6)
    for dim, shards_of in split:
        steps = jnp.exp(jax.random.uniform(jax.random.fold_in(own, dim), (shards_of,), jnp.float32, low / len(split), top_value / len(split)))
        level = level * jnp.repeat(steps, dims[dim] // shards_of).reshape([-1 if axis == dim else 1 for axis in range(len(dims))])
    return level


def split_up(amount, total, limit, slope):
    weights = [(1 << 20) // math.isqrt(rank ** slope) + 1 for rank in range(2, amount + 1)]
    surplus, counts = total - limit - (amount - 1), [1] * (amount - 1)
    while surplus > 0:
        free = [i for i in range(amount - 1) if counts[i] < limit]
        mass, left = sum([weights[i] for i in free]), surplus
        for i in free:
            more = min(limit - counts[i], max(1, left * weights[i] // mass), surplus)
            counts[i] = counts[i] + more
            surplus = surplus - more
    return np.array([limit] + counts)


def ragged_sizes(key, amount, total, reach, lean):
    if amount == 2:
        one = jax.random.randint(key, (), max(1, total - reach), min(reach, total - 1) + 1)
        return jnp.stack([one, total - one])
    lengths = jnp.asarray(split_up(amount, total, reach, lean), jnp.int32)
    couples = (amount - 1) // 2
    source_of, receiver = lengths[1:1 + 2 * couples:2], lengths[2:2 + 2 * couples:2]
    margin = jnp.minimum(source_of - 1, reach - receiver)
    passed = jax.random.randint(jax.random.fold_in(key, 1), (couples,), 0, 1 << 20) % (margin + 1)
    lengths = lengths.at[1:1 + 2 * couples:2].set(source_of - passed).at[2:2 + 2 * couples:2].set(receiver + passed)
    return lengths[jax.random.permutation(jax.random.fold_in(key, 2), amount)]


def centred(stream_key, shape, width, bound, pieces=(), kind=jnp.bfloat16):
    gain = steps_of(stream_key, shape, pieces, -0.22, 0.18) if pieces else 1.0
    result = jax.random.normal(stream_key, shape, jnp.float32) * width * gain
    return jnp.minimum(jnp.maximum(result, -bound), bound).astype(kind)


def setup_inputs(seed: int = 0) -> dict:
    streams_of = jax.random.split(jax.random.key(seed), 8)
    return {
        "image_embed": centred(streams_of[0], (TOKENS, EMBED), 1.0, 6.0, ((0, 128),)),
        "text_embed": centred(streams_of[1], (TOKENS, EMBED), 1.0, 6.0, ((0, 128),)),
        "image_head": centred(streams_of[2], (EMBED, PROJ), EMBED ** -0.5, 0.1875),
        "text_head": centred(streams_of[3], (EMBED, PROJ), EMBED ** -0.5, 0.1875),
        "pair_ids": jnp.searchsorted(jnp.cumsum(ragged_sizes(streams_of[4], TOKENS // 4, TOKENS, 8, 0)), jnp.arange(TOKENS), side="right").astype(jnp.int32),
        "logit_scale": jnp.clip(jnp.exp(jax.random.uniform(streams_of[5], (1,), jnp.float32, math.log(8.0), math.log(24.0))), 8.0, 24.0),
        "logit_bias": jnp.clip(jax.random.uniform(streams_of[6], (1,), jnp.float32, -4.0, -1.5), -4.0, -1.5),
    }


def unit_rows(projected):
    length = jnp.sqrt(lax.optimization_barrier(jnp.sum(projected * projected, axis=1, keepdims=True)) + 1e-06)
    return (projected / length, length)

def unit_back(gradient, direction, length):
    radial = lax.optimization_barrier(jnp.sum(gradient * direction, axis=1, keepdims=True))
    return ((gradient - radial * direction) / length).astype(jnp.bfloat16)

def reference(image_embed, text_embed, image_head, text_head, pair_ids, logit_scale, logit_bias):
    loss_weight = 1.0 / math.sqrt(TOKENS)
    scale_value = logit_scale[0]
    bias_value = logit_bias[0]
    img_dir, img_length = unit_rows(jnp.dot(image_embed, image_head, preferred_element_type=jnp.float32))
    txt_dir, txt_length = unit_rows(jnp.dot(text_embed, text_head, preferred_element_type=jnp.float32))
    img_unit = img_dir.astype(jnp.bfloat16)
    txt_unit = txt_dir.astype(jnp.bfloat16)
    blk_rows = TOK_DEV * N_INNER
    blk_count = TOKENS // blk_rows
    img_blocks = img_unit.reshape(blk_count, blk_rows, PROJ)
    id_blocks = pair_ids.reshape(blk_count, blk_rows)

    def visit_block(txt_acc, block_pair):
        units_here, ids_here = block_pair
        logits = scale_value * jnp.dot(units_here, txt_unit.T, preferred_element_type=jnp.float32) + bias_value
        label_sign = jnp.where(ids_here[:, None] == pair_ids[None, :], 1.0, -1.0).astype(logits.dtype)
        pair_coef = (-label_sign * jax.nn.sigmoid(-label_sign * logits) * scale_value * loss_weight).astype(jnp.bfloat16)
        img_part = jnp.dot(pair_coef, txt_unit, preferred_element_type=jnp.float32)
        txt_acc = txt_acc + jnp.dot(pair_coef.T, units_here, preferred_element_type=jnp.float32)
        return (txt_acc, img_part)
    txt_grad, img_parts = lax.scan(visit_block, jnp.zeros((TOKENS, PROJ), jnp.float32), (img_blocks, id_blocks))
    img_grad = img_parts.reshape(TOKENS, PROJ)
    img_back = unit_back(img_grad, img_dir, img_length)
    txt_back = unit_back(txt_grad, txt_dir, txt_length)
    grad_image_head = jnp.dot(image_embed.T, img_back, preferred_element_type=jnp.float32)
    grad_text_head = jnp.dot(text_embed.T, txt_back, preferred_element_type=jnp.float32)
    return (grad_image_head, grad_text_head)
```

```python
import math

import jax
import jax.numpy as jnp
from jax import lax
from jax.sharding import Mesh, PartitionSpec as P

AXES = ("zl", "y", "c", "x", "zh")
SIZES = (2, 4, 2, 4, 2)
BF16 = jnp.bfloat16
F32 = jnp.float32


def routes(move):
    pairs = []
    index = 0
    for zl in range(2):
        for y in range(4):
            for c in range(2):
                for x in range(4):
                    for zh in range(2):
                        tzl, ty, tc, tx, tzh = move(zl, y, c, x, zh)
                        pairs.append((index, (((tzl * 4 + ty) * 2 + tc) * 4 + tx) * 2 + tzh))
                        index += 1
    return pairs


def send(value, move):
    return lax.ppermute(value, AXES, routes(move))


def other_core(zl, y, c, x, zh):
    return (zl, y, 1 - c, x, zh)


def z_pair(swap):
    def move(zl, y, c, x, zh):
        return (1 - zl, y, c, x, zh if (c ^ swap) == 0 else 1 - zh)

    return move


def ring(by, swap):
    def move(zl, y, c, x, zh):
        if (c ^ swap) == 0:
            return (zl, y, c, (x + by) % 4, zh)
        return (zl, (y + by) % 4, c, x, zh)

    return move


def z_ring(by):
    def move(zl, y, c, x, zh):
        z = (zh * 2 + zl + by) % 4
        return (z % 2, y, c, x, z // 2)

    return move


def with_partner(value, swap):
    got = send(value, z_pair(swap))
    return jnp.concatenate([value[:128], got[:128], value[128:129], got[128:129], value[130:144]], axis=0)


def unit_rows(projected):
    length = jnp.sqrt(jnp.sum(projected * projected, axis=1, keepdims=True) + 1e-06)
    return (projected / length, length)


def block_ids(blocks):
    rows = jnp.concatenate([block[256:258, :256].astype(F32) for block in blocks], axis=0)
    return (rows[:, :128] * 64.0 + rows[:, 128:]).reshape(-1)


def scattered(value, by_route, mine, kind):
    rows = value.shape[0] // 4
    total = lax.dynamic_slice_in_dim(value, mine * rows, rows, 0)
    parts = []
    for by in (1, 3, 2):
        part = lax.dynamic_slice_in_dim(value, lax.rem(mine + by, 4) * rows, rows, 0).astype(kind)
        parts.append(send(part, by_route(by)))
    for part in parts:
        total = total + part.astype(F32)
    return total


def gathered(value, by_route, mine):
    rows = value.shape[0]
    out = jnp.zeros((4 * rows,) + value.shape[1:], value.dtype)
    parts = [(0, value)] + [(by, send(value, by_route(by))) for by in (1, 3, 2)]
    for by, part in parts:
        out = lax.dynamic_update_slice_in_dim(out, part, lax.rem(mine + 4 - by, 4) * rows, 0)
    return out


def local(image_embed, text_embed, image_head, text_head, pair_ids, logit_scale, logit_bias):
    core = lax.axis_index("c")
    first = core == 0
    scale = logit_scale[0]
    bias = logit_bias[0]
    weight = 1.0 / math.sqrt(16384)

    ids_row = jnp.concatenate(
        [(pair_ids // 64).astype(BF16), (pair_ids % 64).astype(BF16), jnp.zeros((896,), BF16)]
    )[None]
    ids_rows = jnp.concatenate([ids_row, jnp.zeros((15, 1152), BF16)], axis=0)
    mine = jnp.concatenate([jnp.where(first, image_embed, text_embed), ids_rows], axis=0)
    theirs = jnp.concatenate([jnp.where(first, text_embed, image_embed), ids_rows], axis=0)
    head_mine = jnp.where(first, image_head, text_head)
    head_theirs = jnp.where(first, text_head, image_head)

    mine = with_partner(mine, 0)
    theirs = with_partner(theirs, 1)
    mine_blocks = [mine]
    theirs_blocks = [theirs]
    for by in (1, 3, 2):
        mine_blocks.append(send(mine, ring(by, 0)))
        theirs_blocks.append(send(theirs, ring(by, 1)))
    mine_over = [send(block, other_core) for block in theirs_blocks]
    theirs_over = [send(block, other_core) for block in mine_blocks]
    mine_blocks = mine_blocks + mine_over
    theirs_blocks = theirs_blocks + theirs_over

    rows_mine = jnp.concatenate([block[:256] for block in mine_blocks], axis=0)
    rows_theirs = jnp.concatenate([block[:256] for block in theirs_blocks], axis=0)
    ids_mine = block_ids(mine_blocks)
    ids_theirs = block_ids(theirs_blocks)

    dir_mine, length_mine = unit_rows(jnp.dot(rows_mine, head_mine, preferred_element_type=F32))
    dir_theirs, _ = unit_rows(jnp.dot(rows_theirs, head_theirs, preferred_element_type=F32))
    unit_mine = dir_mine.astype(BF16)
    unit_theirs = dir_theirs.astype(BF16)
    logits = (
        scale
        * lax.dot_general(
            unit_mine, unit_theirs, (((1,), (1,)), ((), ())), preferred_element_type=F32
        )
        + bias
    )
    sign = jnp.where(ids_mine[:, None] == ids_theirs[None, :], 1.0, -1.0)
    coef = (-sign * jax.nn.sigmoid(-sign * logits) * scale * weight).astype(BF16)
    grad = jnp.dot(coef, unit_theirs, preferred_element_type=F32)
    radial = jnp.sum(grad * dir_mine, axis=1, keepdims=True)
    back = ((grad - radial * dir_mine) / length_mine).astype(BF16)
    part = lax.dot_general(rows_mine, back, (((0,), (0,)), ((), ())), preferred_element_type=F32)

    at_x = lax.axis_index("x")
    at_y = lax.axis_index("y")
    at_first = jnp.where(first, at_x, at_y)
    at_second = jnp.where(first, at_y, at_x)
    part = scattered(part, lambda by: ring(by, 0), at_first, BF16)
    part = scattered(part, lambda by: ring(by, 1), at_second, F32)
    moved = [send(part, z_ring(by)) for by in (1, 3, 2)]
    at_z = lax.axis_index("zh") * 2 + lax.axis_index("zl")
    stack = jnp.zeros((4,) + part.shape, F32)
    for by, piece in zip((0, 1, 3, 2), [part] + moved):
        stack = lax.dynamic_update_slice_in_dim(stack, piece[None], lax.rem(at_z + 4 - by, 4), 0)
    part = (stack[0] + stack[1]) + (stack[2] + stack[3])
    part = gathered(part, lambda by: ring(by, 1), at_second)
    whole = gathered(part, lambda by: ring(by, 0), at_first)
    other = send(whole, other_core)
    return (jnp.where(first, whole, other), jnp.where(first, other, whole))


def solution(mesh):
    split = Mesh(mesh.devices.reshape(SIZES), AXES)
    every = P(AXES)
    return jax.shard_map(
        local,
        mesh=split,
        in_specs=(every, every, P(), P(), every, P(), P()),
        out_specs=(P(), P()),
        check_vma=False,
    )
```

```python
import math

import jax
import jax.numpy as jnp
from jax import lax
from jax.experimental import pallas as pl
from jax.experimental.pallas import tpu as pltpu
from jax.sharding import Mesh, PartitionSpec as P

AXES = ("zl", "y", "c", "x", "zh")
SIZES = (2, 4, 2, 4, 2)
BF16 = jnp.bfloat16
F32 = jnp.float32
WIDE = 1152
ROWS = 2048
VMEM_BYTES = 58 * 1024 * 1024


def routes(move):
    pairs = []
    index = 0
    for zl in range(2):
        for y in range(4):
            for c in range(2):
                for x in range(4):
                    for zh in range(2):
                        tzl, ty, tc, tx, tzh = move(zl, y, c, x, zh)
                        pairs.append((index, (((tzl * 4 + ty) * 2 + tc) * 4 + tx) * 2 + tzh))
                        index += 1
    return pairs


def send(value, move):
    return lax.ppermute(value, AXES, routes(move))


def other_core(zl, y, c, x, zh):
    return (zl, y, 1 - c, x, zh)


def z_pair(swap):
    def move(zl, y, c, x, zh):
        return (1 - zl, y, c, x, zh if (c ^ swap) == 0 else 1 - zh)

    return move


def ring(by, swap):
    def move(zl, y, c, x, zh):
        if (c ^ swap) == 0:
            return (zl, y, c, (x + by) % 4, zh)
        return (zl, (y + by) % 4, c, x, zh)

    return move


def z_ring(by):
    def move(zl, y, c, x, zh):
        z = (zh * 2 + zl + by) % 4
        return (z % 2, y, c, x, z // 2)

    return move


def with_partner(value, swap):
    got = send(value, z_pair(swap))
    return jnp.concatenate([value[:128], got[:128], value[128:129], got[128:129], value[130:144]], axis=0)


def rows_of_ids(block_ref):
    coded = block_ref[256:272, :256].astype(F32)
    parts = [coded[i : i + 1, :128] * 64.0 + coded[i : i + 1, 128:] for i in range(2)]
    return jnp.broadcast_to(jnp.concatenate(parts, axis=1), (8, 256))


def project_kernel(*refs):
    own, over, own_far, over_far, head_mine, head_theirs = refs[:6]
    proj, unit, rows, ids_mine, ids_theirs = refs[-5:]
    for part, (near, far) in enumerate(((own, own_far), (over, over_far))):
        at = pl.ds(part * 256, 256)
        block = near[:256, :]
        rows[at, :] = block
        proj[at, :] = jnp.dot(block, head_mine[...], preferred_element_type=F32)
        other = jnp.dot(far[:256, :], head_theirs[...], preferred_element_type=F32)
        length = jnp.sqrt(jnp.sum(other * other, axis=1, keepdims=True) + 1e-06)
        unit[at, :] = (other / length).astype(BF16)
        ids_mine[part * 8 : part * 8 + 8, :] = rows_of_ids(near)
        ids_theirs[part * 8 : part * 8 + 8, :] = rows_of_ids(far)


def project(turn, blocks, heads, held):
    whole = pl.BlockSpec(memory_space=pltpu.VMEM)
    shapes = [
        jax.ShapeDtypeStruct((ROWS, WIDE), F32),
        jax.ShapeDtypeStruct((ROWS, WIDE), BF16),
        jax.ShapeDtypeStruct((ROWS, WIDE), BF16),
        jax.ShapeDtypeStruct((64, 256), F32),
        jax.ShapeDtypeStruct((64, 256), F32),
    ]
    return pl.pallas_call(
        project_kernel,
        grid=(1,),
        out_shape=shapes,
        in_specs=[whole] * 6 + [pl.BlockSpec(memory_space=pl.ANY)] * len(held),
        out_specs=[pl.BlockSpec((512, WIDE), lambda i: (turn, 0))] * 3
        + [pl.BlockSpec((16, 256), lambda i: (turn, 0))] * 2,
        input_output_aliases={6 + i: i for i in range(len(held))},
        compiler_params=pltpu.CompilerParams(vmem_limit_bytes=40 * 1024 * 1024),
        cost_estimate=pl.CostEstimate(
            flops=2 * 1024 * WIDE * WIDE, bytes_accessed=12_000_000, transcendentals=0
        ),
        name="project",
    )(*blocks, *heads, *held)


def pair_kernel(
    at_ref, knob_ref, proj, rows, ids_mine, unit, ids_theirs, own, one, three, two, total, coef
):
    step = pl.program_id(0)
    half_scale, half_bias, half = knob_ref[0], knob_ref[1], knob_ref[2]
    projected = proj[...]
    length = jnp.sqrt(jnp.sum(projected * projected, axis=1, keepdims=True) + 1e-06)
    near = (projected / length).astype(BF16)
    eye = lax.broadcasted_iota(jnp.int32, (256, 256), 0) == lax.broadcasted_iota(
        jnp.int32, (256, 256), 1
    )
    columns = [
        jnp.sum(jnp.where(eye, ids_mine[i * 8 : i * 8 + 1, :], 0.0), axis=1, keepdims=True)
        for i in range(2)
    ]
    column = jnp.concatenate(columns, axis=0)
    for part in range(8):
        at = pl.ds(part * 256, 256)
        cosine = lax.dot_general(
            near, unit[at, :], (((1,), (1,)), ((), ())), preferred_element_type=F32
        )
        base = jnp.where(column == ids_theirs[part * 8 : part * 8 + 1, :], -half, half)
        coef[:, at] = (jnp.tanh(cosine * half_scale + half_bias) * half + base).astype(BF16)
    grad = jnp.dot(coef[...], unit[...], preferred_element_type=F32)
    direction = proj[...] / length
    radial = jnp.sum(grad * direction, axis=1, keepdims=True)
    back = ((grad - radial * direction) / length).astype(BF16)
    part = lax.dot_general(
        rows[...], back, (((0,), (0,)), ((), ())), preferred_element_type=F32
    )

    @pl.when(step == 0)
    def _():
        total[...] = part

    @pl.when(step > 0)
    def _():
        total[...] += part

    @pl.when(step == 3)
    def _():
        for by, out in ((0, own), (1, one), (3, three), (2, two)):
            place = pl.multiple_of(lax.rem(at_ref[0] + by, 4) * 288, 288)
            out[...] = total[pl.ds(place, 288), :].astype(out.dtype)


def pair_tile(at, knobs, held):
    proj, unit, rows, ids_mine, ids_theirs = held
    fixed = lambda i: (0, 0)
    moving = lambda i: (i, 0)
    smem = pl.BlockSpec(memory_space=pltpu.SMEM)
    return pl.pallas_call(
        pair_kernel,
        grid=(4,),
        out_shape=[jax.ShapeDtypeStruct((288, WIDE), kind) for kind in (F32, BF16, BF16, BF16)],
        in_specs=[
            smem,
            smem,
            pl.BlockSpec((512, WIDE), moving),
            pl.BlockSpec((512, WIDE), moving),
            pl.BlockSpec((16, 256), moving),
            pl.BlockSpec((ROWS, WIDE), fixed, pipeline_mode=pl.Buffered(1)),
            pl.BlockSpec((64, 256), fixed),
        ],
        out_specs=[pl.BlockSpec((288, WIDE), fixed)] * 4,
        scratch_shapes=[pltpu.VMEM((WIDE, WIDE), F32), pltpu.VMEM((512, ROWS), BF16)],
        compiler_params=pltpu.CompilerParams(
            dimension_semantics=("arbitrary",), vmem_limit_bytes=VMEM_BYTES
        ),
        cost_estimate=pl.CostEstimate(
            flops=2 * ROWS * WIDE * (2 * ROWS + WIDE),
            bytes_accessed=24_000_000,
            transcendentals=ROWS * ROWS,
        ),
        name="pair_tile",
    )(at, knobs, proj, rows, ids_mine, unit, ids_theirs)


def place_kernel(where_ref, *refs):
    pieces, outs = refs[:8], refs[8:10]
    narrow, wide, in_sems, out_sems = refs[10:]
    loads = [
        pltpu.make_async_copy(piece, narrow.at[i], in_sems.at[i]) for i, piece in enumerate(pieces)
    ]
    for load in loads:
        load.start()

    def stores(i):
        head = where_ref[0] if i < 4 else 1 - where_ref[0]
        row = pl.multiple_of(where_ref[1 + i] * 288, 288)
        for h in range(2):
            copy = pltpu.make_async_copy(
                wide.at[i], outs[h].at[pl.ds(row, 288), :], out_sems.at[i]
            )
            yield head == h, copy

    for i in range(8):
        loads[i].wait()
        wide[i] = narrow[i].astype(F32)
        for here, copy in stores(i):
            pl.when(here)(copy.start)
    for i in range(8):
        for here, copy in stores(i):
            pl.when(here)(copy.wait)


def place(where, pieces):
    return pl.pallas_call(
        place_kernel,
        out_shape=[jax.ShapeDtypeStruct((WIDE, WIDE), F32)] * 2,
        in_specs=[pl.BlockSpec(memory_space=pltpu.SMEM)]
        + [pl.BlockSpec(memory_space=pl.ANY)] * 8,
        out_specs=[pl.BlockSpec(memory_space=pl.ANY)] * 2,
        scratch_shapes=[
            pltpu.VMEM((8, 288, WIDE), BF16),
            pltpu.VMEM((8, 288, WIDE), F32),
            pltpu.SemaphoreType.DMA((8,)),
            pltpu.SemaphoreType.DMA((8,)),
        ],
        compiler_params=pltpu.CompilerParams(vmem_limit_bytes=VMEM_BYTES),
        name="place",
    )(where, *pieces)


def added(total, parts):
    for part in parts:
        total = total + part.astype(F32)
    return total


def scattered(value, by_route, mine):
    rows = value.shape[0] // 4
    total = lax.dynamic_slice_in_dim(value, mine * rows, rows, 0)
    parts = []
    for by in (1, 3, 2):
        part = lax.dynamic_slice_in_dim(value, lax.rem(mine + by, 4) * rows, rows, 0)
        parts.append(send(part, by_route(by)))
    return added(total, parts)


def local(image_embed, text_embed, image_head, text_head, pair_ids, logit_scale, logit_bias):
    first = lax.axis_index("c") == 0
    scale = logit_scale[0]
    half = scale * (0.5 / math.sqrt(16384))
    knobs = jnp.stack([scale * 0.5, logit_bias[0] * 0.5, half])

    ids_row = jnp.concatenate(
        [(pair_ids // 64).astype(BF16), (pair_ids % 64).astype(BF16), jnp.zeros((896,), BF16)]
    )[None]
    ids_rows = jnp.concatenate([ids_row, jnp.zeros((15, WIDE), BF16)], axis=0)
    mine = jnp.concatenate([jnp.where(first, image_embed, text_embed), ids_rows], axis=0)
    theirs = jnp.concatenate([jnp.where(first, text_embed, image_embed), ids_rows], axis=0)
    heads = (jnp.where(first, image_head, text_head), jnp.where(first, text_head, image_head))

    mine = with_partner(mine, 0)
    theirs = with_partner(theirs, 1)
    held = ()
    for turn, by in enumerate((0, 1, 3, 2)):
        own = mine if by == 0 else send(mine, ring(by, 0))
        own_far = theirs if by == 0 else send(theirs, ring(by, 1))
        over, over_far = send(own_far, other_core), send(own, other_core)
        held = project(turn, (own, over, own_far, over_far), heads, held)

    at_x = lax.axis_index("x")
    at_y = lax.axis_index("y")
    at_first = jnp.where(first, at_x, at_y)
    at_second = jnp.where(first, at_y, at_x)
    part, *away = pair_tile(at_first[None], knobs, held)
    part = added(part, [send(piece, ring(by, 0)) for by, piece in zip((1, 3, 2), away)])
    part = scattered(part, lambda by: ring(by, 1), at_second)
    moved = [send(part, z_ring(by)) for by in (1, 3, 2)]
    at_z = lax.axis_index("zh") * 2 + lax.axis_index("zl")
    stack = jnp.zeros((4,) + part.shape, F32)
    for by, piece in zip((0, 1, 3, 2), [part] + moved):
        stack = lax.dynamic_update_slice_in_dim(stack, piece[None], lax.rem(at_z + 4 - by, 4), 0)
    part = ((stack[0] + stack[1]) + (stack[2] + stack[3])).astype(BF16)

    quarter = jnp.zeros((288, WIDE), BF16)
    for by in (0, 1, 3, 2):
        piece = part if by == 0 else send(part, ring(by, 1))
        quarter = lax.dynamic_update_slice_in_dim(
            quarter, piece, lax.rem(at_second + 4 - by, 4) * 72, 0
        )
    pieces = [quarter] + [send(quarter, ring(by, 0)) for by in (1, 3, 2)]
    pieces = pieces + [send(piece, other_core) for piece in pieces]
    where = [lax.axis_index("c")]
    for at in (at_first, at_second):
        where += [lax.rem(at + 4 - by, 4) for by in (0, 1, 3, 2)]
    return tuple(place(jnp.stack(where).astype(jnp.int32), pieces))


def solution(mesh):
    split = Mesh(mesh.devices.reshape(SIZES), AXES)
    every = P(AXES)
    return jax.shard_map(
        local,
        mesh=split,
        in_specs=(every, every, P(), P(), every, P(), P()),
        out_specs=(P(), P()),
        check_vma=False,
    )
```

```python
import functools
import math

import jax
import jax.numpy as jnp
from jax import lax
from jax.experimental import pallas as pl
from jax.experimental.pallas import tpu as pltpu
from jax.sharding import Mesh, PartitionSpec as P

AXES = ("zl", "y", "c", "x", "zh")
SIZES = (2, 4, 2, 4, 2)
BF16 = jnp.bfloat16
F32 = jnp.float32
WIDE = 1152
ROWS = 2048
VMEM_BYTES = 58 * 1024 * 1024


def routes(move):
    pairs = []
    index = 0
    for zl in range(2):
        for y in range(4):
            for c in range(2):
                for x in range(4):
                    for zh in range(2):
                        tzl, ty, tc, tx, tzh = move(zl, y, c, x, zh)
                        pairs.append((index, (((tzl * 4 + ty) * 2 + tc) * 4 + tx) * 2 + tzh))
                        index += 1
    return pairs


def send(value, move):
    return lax.ppermute(value, AXES, routes(move))


def other_core(zl, y, c, x, zh):
    return (zl, y, 1 - c, x, zh)


def z_pair(swap):
    def move(zl, y, c, x, zh):
        return (1 - zl, y, c, x, zh if (c ^ swap) == 0 else 1 - zh)

    return move


def ring(by, swap):
    def move(zl, y, c, x, zh):
        if (c ^ swap) == 0:
            return (zl, y, c, (x + by) % 4, zh)
        return (zl, (y + by) % 4, c, x, zh)

    return move


def z_ring(by):
    def move(zl, y, c, x, zh):
        z = (zh * 2 + zl + by) % 4
        return (z % 2, y, c, x, z // 2)

    return move


def with_partner(value, swap):
    got = send(value, z_pair(swap))
    return jnp.concatenate([value[:128], got[:128], value[128:129], got[128:129], value[130:144]], axis=0)


def eye_256():
    return lax.broadcasted_iota(jnp.int32, (256, 256), 0) == lax.broadcasted_iota(
        jnp.int32, (256, 256), 1
    )


def as_column(row):
    return jnp.sum(jnp.where(eye_256(), row, 0.0), axis=1, keepdims=True)


def id_row(coded):
    coded = coded.astype(F32)
    parts = [coded[i : i + 1, :128] * 64.0 + coded[i : i + 1, 128:256] for i in range(2)]
    return jnp.concatenate(parts, axis=1)


def project_kernel(near, far, head_mine, head_theirs, unit_near, unit_far, inv_near, inv_far):
    sides = ((near, head_mine, unit_near, inv_near), (far, head_theirs, unit_far, inv_far))
    for block, head, unit, inv in sides:
        projected = jnp.dot(block[:256, :], head[...], preferred_element_type=F32)
        inverse = lax.rsqrt(jnp.sum(projected * projected, axis=1, keepdims=True) + 1e-06)
        unit[:256, :] = (projected * inverse).astype(BF16)
        unit[256:, :] = block[256:, :]
        row = jnp.sum(jnp.where(eye_256(), inverse, 0.0), axis=0, keepdims=True)
        inv[...] = jnp.broadcast_to(row, (8, 256))


def project(near, far, heads):
    whole = pl.BlockSpec(memory_space=pltpu.VMEM)
    return pl.pallas_call(
        project_kernel,
        out_shape=[jax.ShapeDtypeStruct((272, WIDE), BF16)] * 2
        + [jax.ShapeDtypeStruct((8, 256), F32)] * 2,
        in_specs=[whole] * 4,
        out_specs=[whole] * 4,
        compiler_params=pltpu.CompilerParams(vmem_limit_bytes=24 * 1024 * 1024),
        cost_estimate=pl.CostEstimate(
            flops=2 * 512 * WIDE * WIDE, bytes_accessed=8_000_000, transcendentals=0
        ),
        name="project",
    )(near, far, *heads)


def unit_loads(sources, units, ids, unit_sems, id_sems):
    loads = []
    for i, source in enumerate(sources):
        rows = source.at[pl.ds(0, 256), :]
        coded = source.at[pl.ds(256, 16), pl.ds(0, 256)]
        loads.append(
            (
                pltpu.make_async_copy(rows, units.at[pl.ds(i * 256, 256), :], unit_sems.at[i]),
                pltpu.make_async_copy(coded, ids.at[i], id_sems.at[i]),
            )
        )
    return loads


def pair_coefs(knob_ref, near, column, unit, ids, coef, parts):
    half_scale, half_bias, half = knob_ref[0], knob_ref[1], knob_ref[2]
    for part in parts:
        cosine = lax.dot_general(
            near,
            unit[part * 256 : part * 256 + 256, :],
            (((1,), (1,)), ((), ())),
            preferred_element_type=F32,
        )
        base = jnp.where(column == id_row(ids[part]), -half, half)
        value = jnp.tanh(cosine * half_scale + half_bias) * half + base
        coef[:, pl.ds(part * 256, 256)] = value.astype(BF16)


def chunk_column(ids, step):
    return jnp.concatenate([as_column(id_row(ids[2 * step + i])) for i in range(2)], axis=0)


def early_kernel(knob_ref, *refs):
    sources, grad = refs[:12], refs[12]
    near, near_ids, far, far_ids, coef, sems = refs[13:]
    step = pl.program_id(0)
    near_loads = unit_loads(sources[:6], near, near_ids, sems.at[0], sems.at[1])
    far_loads = unit_loads(sources[6:], far, far_ids, sems.at[2], sems.at[3])

    @pl.when(step == 0)
    def _():
        for pair in far_loads + near_loads:
            for load in pair:
                load.start()
        for pair in far_loads:
            for load in pair:
                load.wait()

    for i, pair in enumerate(near_loads):

        @pl.when(step == i // 2)
        def _(pair=pair):
            for load in pair:
                load.wait()

    rows = near[pl.ds(pl.multiple_of(step * 512, 512), 512), :]
    pair_coefs(knob_ref, rows, chunk_column(near_ids, step), far, far_ids, coef, range(6))
    grad[...] = jnp.dot(coef[...], far[...], preferred_element_type=F32)


def early_pairs(knobs, near, far):
    return pl.pallas_call(
        early_kernel,
        grid=(3,),
        out_shape=jax.ShapeDtypeStruct((1536, WIDE), F32),
        in_specs=[pl.BlockSpec(memory_space=pltpu.SMEM)]
        + [pl.BlockSpec(memory_space=pltpu.HBM)] * 12,
        out_specs=pl.BlockSpec((512, WIDE), lambda i: (i, 0)),
        scratch_shapes=[
            pltpu.VMEM((1536, WIDE), BF16),
            pltpu.VMEM((6, 16, 256), BF16),
            pltpu.VMEM((1536, WIDE), BF16),
            pltpu.VMEM((6, 16, 256), BF16),
            pltpu.VMEM((512, 1536), BF16),
            pltpu.SemaphoreType.DMA((4, 6)),
        ],
        compiler_params=pltpu.CompilerParams(
            dimension_semantics=("arbitrary",), vmem_limit_bytes=40 * 1024 * 1024
        ),
        cost_estimate=pl.CostEstimate(
            flops=4 * 1536 * 1536 * WIDE, bytes_accessed=14_000_000, transcendentals=1536 * 1536
        ),
        name="early_pairs",
    )(knobs, *near, *far)


def late_kernel(at_ref, knob_ref, grad, *refs):
    sources, outs = refs[:32], refs[32:36]
    near, near_ids, far, far_ids, rows, inv, coef, total, sems, more_sems = refs[36:]
    step = pl.program_id(0)
    near_loads = unit_loads(sources[:8], near, near_ids, sems.at[0], sems.at[1])
    far_loads = unit_loads(sources[8:16], far, far_ids, sems.at[2], sems.at[3])
    for i in range(8):
        near_loads[i] += (
            pltpu.make_async_copy(
                sources[16 + i].at[pl.ds(0, 256), :],
                rows.at[pl.ds(i * 256, 256), :],
                more_sems.at[0, i],
            ),
            pltpu.make_async_copy(sources[24 + i], inv.at[i], more_sems.at[1, i]),
        )

    @pl.when(step == 0)
    def _():
        for pair in far_loads[6:] + near_loads + far_loads[:6]:
            for load in pair:
                load.start()
        for pair in far_loads[6:]:
            for load in pair:
                load.wait()
        total[...] = jnp.zeros_like(total)

    for i, pair in enumerate(near_loads):

        @pl.when(step == i // 2)
        def _(pair=pair):
            for load in pair:
                load.wait()

    at = pl.ds(pl.multiple_of(step * 512, 512), 512)
    column = chunk_column(near_ids, step)
    inverse = jnp.concatenate([as_column(inv[2 * step + i][:1]) for i in range(2)], axis=0)

    def finish(gradient):
        direction = near[at, :].astype(F32)
        radial = jnp.sum(gradient * direction, axis=1, keepdims=True)
        back = ((gradient - radial * direction) * inverse).astype(BF16)
        total[...] += lax.dot_general(
            rows[at, :], back, (((0,), (0,)), ((), ())), preferred_element_type=F32
        )

    @pl.when(step < 3)
    def _():
        pair_coefs(knob_ref, near[at, :], column, far, far_ids, coef, (6, 7))
        finish(
            grad[...]
            + jnp.dot(coef[:, 1536:], far[1536:, :], preferred_element_type=F32)
        )

    @pl.when(step == 3)
    def _():
        for pair in far_loads[:6]:
            for load in pair:
                load.wait()
        pair_coefs(knob_ref, near[at, :], column, far, far_ids, coef, range(8))
        finish(jnp.dot(coef[...], far[...], preferred_element_type=F32))
        for by, out in zip((0, 1, 3, 2), outs):
            place = pl.multiple_of(lax.rem(at_ref[0] + by, 4) * 288, 288)
            out[...] = total[pl.ds(place, 288), :].astype(out.dtype)


def late_pairs(at, knobs, grad, near, far, rows, inv):
    smem = pl.BlockSpec(memory_space=pltpu.SMEM)
    return pl.pallas_call(
        late_kernel,
        grid=(4,),
        out_shape=[jax.ShapeDtypeStruct((288, WIDE), kind) for kind in (F32, BF16, BF16, BF16)],
        in_specs=[smem, smem, pl.BlockSpec((512, WIDE), lambda i: (jnp.minimum(i, 2), 0))]
        + [pl.BlockSpec(memory_space=pltpu.HBM)] * 32,
        out_specs=[
            pl.BlockSpec((288, WIDE), lambda i: (0, 0), pipeline_mode=pl.Buffered(1))
        ]
        * 4,
        scratch_shapes=[
            pltpu.VMEM((ROWS, WIDE), BF16),
            pltpu.VMEM((8, 16, 256), BF16),
            pltpu.VMEM((ROWS, WIDE), BF16),
            pltpu.VMEM((8, 16, 256), BF16),
            pltpu.VMEM((ROWS, WIDE), BF16),
            pltpu.VMEM((8, 8, 256), F32),
            pltpu.VMEM((512, ROWS), BF16),
            pltpu.VMEM((WIDE, WIDE), F32),
            pltpu.SemaphoreType.DMA((4, 8)),
            pltpu.SemaphoreType.DMA((2, 8)),
        ],
        compiler_params=pltpu.CompilerParams(
            dimension_semantics=("arbitrary",), vmem_limit_bytes=VMEM_BYTES
        ),
        cost_estimate=pl.CostEstimate(
            flops=4 * 7 * 512 * 512 * WIDE + 2 * ROWS * WIDE * WIDE,
            bytes_accessed=25_000_000,
            transcendentals=7 * 512 * 512,
        ),
        name="late_pairs",
    )(at, knobs, grad, *near, *far, *rows, *inv)


def place_kernel(heads, where_ref, *refs):
    count = len(heads)
    pieces, outs = refs[:count], refs[-6:-4]
    narrow, wide, in_sems, out_sems = refs[-4:]
    loads = [
        pltpu.make_async_copy(piece, narrow.at[i], in_sems.at[i]) for i, piece in enumerate(pieces)
    ]
    for load in loads:
        load.start()

    def stores(i):
        head = where_ref[0] if heads[i] == 0 else 1 - where_ref[0]
        row = pl.multiple_of(where_ref[1 + i] * 288, 288)
        for h in range(2):
            copy = pltpu.make_async_copy(
                wide.at[i], outs[h].at[pl.ds(row, 288), :], out_sems.at[i]
            )
            yield head == h, copy

    for i in range(count):
        loads[i].wait()
        wide[i] = narrow[i].astype(F32)
        for here, copy in stores(i):
            pl.when(here)(copy.start)
    for i in range(count):
        for here, copy in stores(i):
            pl.when(here)(copy.wait)


def place(where, heads, pieces, held):
    count = len(pieces)
    hbm = pl.BlockSpec(memory_space=pltpu.HBM)
    return pl.pallas_call(
        functools.partial(place_kernel, heads),
        out_shape=[jax.ShapeDtypeStruct((WIDE, WIDE), F32)] * 2,
        in_specs=[pl.BlockSpec(memory_space=pltpu.SMEM)] + [hbm] * (count + len(held)),
        out_specs=[hbm] * 2,
        input_output_aliases={1 + count + i: i for i in range(len(held))},
        scratch_shapes=[
            pltpu.VMEM((count, 288, WIDE), BF16),
            pltpu.VMEM((count, 288, WIDE), F32),
            pltpu.SemaphoreType.DMA((count,)),
            pltpu.SemaphoreType.DMA((count,)),
        ],
        compiler_params=pltpu.CompilerParams(vmem_limit_bytes=32 * 1024 * 1024),
        cost_estimate=pl.CostEstimate(
            flops=0, bytes_accessed=count * 288 * WIDE * 6, transcendentals=0
        ),
        name="place",
    )(where, *pieces, *held)


def added(total, parts):
    for part in parts:
        total = total + part.astype(F32)
    return total


def scattered(value, by_route, mine):
    rows = value.shape[0] // 4
    total = lax.dynamic_slice_in_dim(value, mine * rows, rows, 0)
    parts = []
    for by in (1, 3, 2):
        part = lax.dynamic_slice_in_dim(value, lax.rem(mine + by, 4) * rows, rows, 0)
        parts.append(send(part, by_route(by)))
    return added(total, parts)


def local(image_embed, text_embed, image_head, text_head, pair_ids, logit_scale, logit_bias):
    first = lax.axis_index("c") == 0
    scale = logit_scale[0]
    half = scale * (0.5 / math.sqrt(16384))
    knobs = jnp.stack([scale * 0.5, logit_bias[0] * 0.5, half])

    ids_row = jnp.concatenate(
        [(pair_ids // 64).astype(BF16), (pair_ids % 64).astype(BF16), jnp.zeros((896,), BF16)]
    )[None]
    ids_rows = jnp.concatenate([ids_row, jnp.zeros((15, WIDE), BF16)], axis=0)
    mine = jnp.concatenate([jnp.where(first, image_embed, text_embed), ids_rows], axis=0)
    theirs = jnp.concatenate([jnp.where(first, text_embed, image_embed), ids_rows], axis=0)
    heads = (jnp.where(first, image_head, text_head), jnp.where(first, text_head, image_head))

    mine = with_partner(mine, 0)
    theirs = with_partner(theirs, 1)
    def to_partner(near, far, projected):
        unit_near, unit_far, _, inv_far = projected
        return [send(value, other_core) for value in (unit_far, unit_near, far, inv_far)]

    blocks = [(mine, theirs)]
    away = [send(block, ring(by, far)) for by in (1, 3) for far, block in enumerate((mine, theirs))]
    projected = [project(mine, theirs, heads)]
    mine, theirs, away, projected = lax.optimization_barrier((mine, theirs, away, projected))
    last = [send(mine, ring(2, 0)), send(theirs, ring(2, 1))]
    blocks = [(mine, theirs), tuple(away[:2]), tuple(away[2:])]
    over = [to_partner(*blocks[0], projected[0])]
    for turn in (1, 2):
        projected.append(project(*blocks[turn], heads))
        over.append(to_partner(*blocks[turn], projected[turn]))

    def gathered_units(turns):
        near, far = [], []
        for turn in range(turns):
            near += [projected[turn][0], over[turn][0]]
            far += [projected[turn][1], over[turn][1]]
        return near, far

    grad = early_pairs(knobs, *gathered_units(3))
    last, grad = lax.optimization_barrier((last, grad))
    blocks.append(tuple(last))
    projected.append(project(*last, heads))
    over.append(to_partner(*last, projected[3]))
    near, far = gathered_units(4)
    rows, inv = [], []
    for turn in range(4):
        rows += [blocks[turn][0], over[turn][2]]
        inv += [projected[turn][2], over[turn][3]]

    at_x = lax.axis_index("x")
    at_y = lax.axis_index("y")
    at_first = jnp.where(first, at_x, at_y)
    at_second = jnp.where(first, at_y, at_x)
    part, *away = late_pairs(at_first[None], knobs, grad, near, far, rows, inv)
    part = added(part, [send(piece, ring(by, 0)) for by, piece in zip((1, 3, 2), away)])
    part = scattered(part, lambda by: ring(by, 1), at_second)
    moved = [send(part, z_ring(by)) for by in (1, 3, 2)]
    at_z = lax.axis_index("zh") * 2 + lax.axis_index("zl")
    stack = jnp.zeros((4,) + part.shape, F32)
    for by, piece in zip((0, 1, 3, 2), [part] + moved):
        stack = lax.dynamic_update_slice_in_dim(stack, piece[None], lax.rem(at_z + 4 - by, 4), 0)
    part = ((stack[0] + stack[1]) + (stack[2] + stack[3])).astype(BF16)

    quarter = jnp.zeros((288, WIDE), BF16)
    for by in (0, 1, 3, 2):
        piece = part if by == 0 else send(part, ring(by, 1))
        quarter = lax.dynamic_update_slice_in_dim(
            quarter, piece, lax.rem(at_second + 4 - by, 4) * 72, 0
        )
    core = lax.axis_index("c")

    def where(bys):
        places = [lax.rem(at + 4 - by, 4) for at in (at_first, at_second) for by in bys]
        return jnp.stack([core] + places).astype(jnp.int32)

    pieces = [quarter] + [send(quarter, ring(by, 0)) for by in (1, 3)]
    pieces = pieces + [send(piece, other_core) for piece in pieces]
    last_piece = send(quarter, ring(2, 0))
    held = place(where((0, 1, 3)), (0, 0, 0, 1, 1, 1), pieces, ())
    last_pieces = [last_piece, send(last_piece, other_core)]
    return tuple(place(where((2,)), (0, 1), last_pieces, held))


def solution(mesh):
    split = Mesh(mesh.devices.reshape(SIZES), AXES)
    every = P(AXES)
    return jax.shard_map(
        local,
        mesh=split,
        in_specs=(every, every, P(), P(), every, P(), P()),
        out_specs=(P(), P()),
        check_vma=False,
    )
```

```python
import functools
import math

import jax
import jax.numpy as jnp
from jax import lax
from jax.experimental import pallas as pl
from jax.experimental.pallas import tpu as pltpu
from jax.sharding import Mesh, PartitionSpec as P

AXES = ("zl", "y", "c", "x", "zh")
SIZES = (2, 4, 2, 4, 2)
BF16 = jnp.bfloat16
F32 = jnp.float32
WIDE = 1152
ROWS = 2048
VMEM_BYTES = 48 * 1024 * 1024


def routes(move):
    pairs = []
    index = 0
    for zl in range(2):
        for y in range(4):
            for c in range(2):
                for x in range(4):
                    for zh in range(2):
                        tzl, ty, tc, tx, tzh = move(zl, y, c, x, zh)
                        pairs.append((index, (((tzl * 4 + ty) * 2 + tc) * 4 + tx) * 2 + tzh))
                        index += 1
    return pairs


def send(value, move):
    return lax.ppermute(value, AXES, routes(move))


def other_core(zl, y, c, x, zh):
    return (zl, y, 1 - c, x, zh)


def z_pair(swap):
    def move(zl, y, c, x, zh):
        return (1 - zl, y, c, x, zh if (c ^ swap) == 0 else 1 - zh)

    return move


def ring(by, swap):
    def move(zl, y, c, x, zh):
        if (c ^ swap) == 0:
            return (zl, y, c, (x + by) % 4, zh)
        return (zl, (y + by) % 4, c, x, zh)

    return move


def z_ring(by):
    def move(zl, y, c, x, zh):
        z = (zh * 2 + zl + by) % 4
        return (z % 2, y, c, x, z // 2)

    return move


def eye_256():
    return lax.broadcasted_iota(jnp.int32, (256, 256), 0) == lax.broadcasted_iota(
        jnp.int32, (256, 256), 1
    )


def as_column(row):
    return jnp.sum(jnp.where(eye_256(), row, 0.0), axis=1, keepdims=True)


def id_row(coded):
    coded = coded.astype(F32)
    parts = [coded[i : i + 1, :128] * 64.0 + coded[i : i + 1, 128:256] for i in (0, 16)]
    return jnp.concatenate(parts, axis=1)


def project_kernel(near, far, head_near, head_far, message, rows_near):
    sides = ((near, head_near, rows_near, 0, 0), (far, head_far, message, 576, 288))
    for block, head, rows, at, to in sides:
        rows[at : at + 256, :] = block[:256, :]
        projected = jnp.dot(block[:256, :], head[...], preferred_element_type=F32)
        inverse = lax.rsqrt(jnp.sum(projected * projected, axis=1, keepdims=True) + 1e-06)
        message[to : to + 256, :] = (projected * inverse).astype(BF16)
        message[to + 256 : to + 288, :] = block[256:288, :]
        rest = jnp.sum(jnp.where(eye_256(), inverse, 0.0), axis=0, keepdims=True)
        lines = lax.broadcasted_iota(jnp.int32, (16, 256), 0)
        coded = block[256:272, :256].astype(F32)
        for line in (1, 2, 3):
            part = rest.astype(BF16).astype(F32)
            coded = jnp.where(lines == line, part, coded)
            rest = rest - part
        message[to + 256 : to + 272, :256] = coded.astype(BF16)


def project(near, far, heads):
    whole = pl.BlockSpec(memory_space=pltpu.VMEM)
    return pl.pallas_call(
        project_kernel,
        out_shape=[
            jax.ShapeDtypeStruct((832, WIDE), BF16),
            jax.ShapeDtypeStruct((256, WIDE), BF16),
        ],
        in_specs=[whole] * 4,
        out_specs=[whole] * 2,
        compiler_params=pltpu.CompilerParams(vmem_limit_bytes=28 * 1024 * 1024),
        cost_estimate=pl.CostEstimate(
            flops=2 * 512 * WIDE * WIDE, bytes_accessed=8_000_000, transcendentals=0
        ),
        name="project",
    )(near, far, *heads)


def unit_loads(sources, units, ids, unit_sems, id_sems):
    loads = []
    for i, (source, start) in enumerate(sources):
        rows = source.at[pl.ds(start, 256), :]
        coded = source.at[pl.ds(start + 256, 32), pl.ds(0, 256)]
        loads.append(
            (
                pltpu.make_async_copy(rows, units.at[pl.ds(i * 256, 256), :], unit_sems.at[i]),
                pltpu.make_async_copy(coded, ids.at[i], id_sems.at[i]),
            )
        )
    return loads


def pair_coefs(knob_ref, near, column, unit, ids, coef, parts):
    half_scale, half_bias, half = knob_ref[0], knob_ref[1], knob_ref[2]
    for part in parts:
        cosine = lax.dot_general(
            near,
            unit[part * 256 : part * 256 + 256, :],
            (((1,), (1,)), ((), ())),
            preferred_element_type=F32,
        )
        base = jnp.where(column == id_row(ids[part]), -half, half)
        value = jnp.tanh(cosine * half_scale + half_bias) * half + base
        coef[:, pl.ds(part * 256, 256)] = value.astype(BF16)


def chunk_column(ids, step):
    return jnp.concatenate([as_column(id_row(ids[2 * step + i])) for i in range(2)], axis=0)


def chunk_inverse(ids, step):
    parts = []
    for i in range(2):
        coded = ids[2 * step + i].astype(F32)
        parts.append(as_column(coded[1:2] + coded[2:3] + coded[3:4]))
    return jnp.concatenate(parts, axis=0)


def unit_sources(own, over):
    near, far = [], []
    for mine, theirs in zip(own, over):
        near += [(mine, 0), (theirs, 288)]
        far += [(mine, 288), (theirs, 0)]
    return near, far


def early_kernel(knob_ref, *refs):
    near_sources, far_sources = unit_sources(refs[:3], refs[3:6])
    grad, near, near_ids, far, far_ids, coef, sems = refs[6:]
    step = pl.program_id(0)
    near_loads = unit_loads(near_sources, near, near_ids, sems.at[0], sems.at[1])
    far_loads = unit_loads(far_sources, far, far_ids, sems.at[2], sems.at[3])

    @pl.when(step == 0)
    def _():
        for pair in far_loads + near_loads:
            for load in pair:
                load.start()
        for pair in far_loads:
            for load in pair:
                load.wait()

    for i, pair in enumerate(near_loads):

        @pl.when(step == i // 2)
        def _(pair=pair):
            for load in pair:
                load.wait()

    rows = near[pl.ds(pl.multiple_of(step * 512, 512), 512), :]
    pair_coefs(knob_ref, rows, chunk_column(near_ids, step), far, far_ids, coef, range(6))
    grad[...] = jnp.dot(coef[...], far[...], preferred_element_type=F32)


def early_pairs(knobs, own, over):
    return pl.pallas_call(
        early_kernel,
        grid=(3,),
        out_shape=jax.ShapeDtypeStruct((1536, WIDE), F32),
        in_specs=[pl.BlockSpec(memory_space=pltpu.SMEM)]
        + [pl.BlockSpec(memory_space=pl.ANY)] * 6,
        out_specs=pl.BlockSpec((512, WIDE), lambda i: (i, 0)),
        scratch_shapes=[
            pltpu.VMEM((1536, WIDE), BF16),
            pltpu.VMEM((6, 32, 256), BF16),
            pltpu.VMEM((1536, WIDE), BF16),
            pltpu.VMEM((6, 32, 256), BF16),
            pltpu.VMEM((512, 1536), BF16),
            pltpu.SemaphoreType.DMA((4, 6)),
        ],
        compiler_params=pltpu.CompilerParams(
            dimension_semantics=("arbitrary",), vmem_limit_bytes=40 * 1024 * 1024
        ),
        cost_estimate=pl.CostEstimate(
            flops=4 * 1536 * 1536 * WIDE, bytes_accessed=14_000_000, transcendentals=1536 * 1536
        ),
        name="early_pairs",
    )(knobs, *own, *over)


def late_kernel(at_ref, knob_ref, early, *refs):
    own, over, own_rows, outs = refs[:4], refs[4:8], refs[8:12], refs[12:16]
    near, near_ids, far, far_ids, rows, grad, coef, total, sems, more_sems = refs[16:]
    near_sources, far_sources = unit_sources(own, over)
    step = pl.program_id(0)
    near_loads = unit_loads(near_sources, near, near_ids, sems.at[0], sems.at[1])
    far_loads = unit_loads(far_sources, far, far_ids, sems.at[2], sems.at[3])
    for i in range(8):
        source = over[i // 2].at[pl.ds(576, 256), :] if i % 2 else own_rows[i // 2]
        near_loads[i] += (
            pltpu.make_async_copy(source, rows.at[pl.ds(i * 256, 256), :], more_sems.at[0, i]),
        )
    for i in range(3):
        near_loads[2 * i] += (
            pltpu.make_async_copy(
                early.at[pl.ds(512 * i, 512), :], grad.at[i], more_sems.at[1, i]
            ),
        )

    @pl.when(step == 0)
    def _():
        for pair in far_loads[6:] + near_loads[:2]:
            for load in pair:
                load.start()
        for pair in far_loads[6:]:
            for load in pair:
                load.wait()
        total[...] = jnp.zeros_like(total)

    for i, pair in enumerate(near_loads):

        @pl.when(step == i // 2)
        def _(pair=pair):
            for load in pair:
                load.wait()

    @pl.when(step == 0)
    def _():
        for pair in near_loads[2:] + far_loads[:6]:
            for load in pair:
                load.start()

    at = pl.ds(pl.multiple_of(step * 512, 512), 512)
    column = chunk_column(near_ids, step)
    inverse = chunk_inverse(near_ids, step)

    def finish(gradient):
        direction = near[at, :].astype(F32)
        radial = jnp.sum(gradient * direction, axis=1, keepdims=True)
        back = ((gradient - radial * direction) * inverse).astype(BF16)
        total[...] += lax.dot_general(
            rows[at, :], back, (((0,), (0,)), ((), ())), preferred_element_type=F32
        )

    @pl.when(step < 3)
    def _():
        pair_coefs(knob_ref, near[at, :], column, far, far_ids, coef, (6, 7))
        more = jnp.dot(coef[:, 1536:], far[1536:, :], preferred_element_type=F32)
        finish(grad[step] + more)

    @pl.when(step == 3)
    def _():
        for pair in far_loads[:6]:
            for load in pair:
                load.wait()
        pair_coefs(knob_ref, near[at, :], column, far, far_ids, coef, range(8))
        finish(jnp.dot(coef[...], far[...], preferred_element_type=F32))
        for by, out in zip((0, 1, 3, 2), outs):
            place = pl.multiple_of(lax.rem(at_ref[0] + by, 4) * 288, 288)
            out[...] = total[pl.ds(place, 288), :].astype(out.dtype)


def late_pairs(at, knobs, early, own, over, own_rows):
    smem = pl.BlockSpec(memory_space=pltpu.SMEM)
    return pl.pallas_call(
        late_kernel,
        grid=(4,),
        out_shape=[jax.ShapeDtypeStruct((288, WIDE), kind) for kind in (F32, BF16, BF16, BF16)],
        in_specs=[smem, smem] + [pl.BlockSpec(memory_space=pl.ANY)] * 13,
        out_specs=[
            pl.BlockSpec((288, WIDE), lambda i: (0, 0), pipeline_mode=pl.Buffered(1))
        ]
        * 4,
        scratch_shapes=[
            pltpu.VMEM((ROWS, WIDE), BF16),
            pltpu.VMEM((8, 32, 256), BF16),
            pltpu.VMEM((ROWS, WIDE), BF16),
            pltpu.VMEM((8, 32, 256), BF16),
            pltpu.VMEM((ROWS, WIDE), BF16),
            pltpu.VMEM((3, 512, WIDE), F32),
            pltpu.VMEM((512, ROWS), BF16),
            pltpu.VMEM((WIDE, WIDE), F32),
            pltpu.SemaphoreType.DMA((4, 8)),
            pltpu.SemaphoreType.DMA((2, 8)),
        ],
        compiler_params=pltpu.CompilerParams(
            dimension_semantics=("arbitrary",), vmem_limit_bytes=VMEM_BYTES
        ),
        cost_estimate=pl.CostEstimate(
            flops=4 * 7 * 512 * 512 * WIDE + 2 * ROWS * WIDE * WIDE,
            bytes_accessed=25_000_000,
            transcendentals=7 * 512 * 512,
        ),
        name="late_pairs",
    )(at, knobs, early, *own, *over, *own_rows)


def place_kernel(heads, where_ref, *refs):
    count = len(heads)
    pieces, outs = refs[:count], refs[-6:-4]
    narrow, wide, in_sems, out_sems = refs[-4:]
    loads = [
        pltpu.make_async_copy(piece, narrow.at[i], in_sems.at[i]) for i, piece in enumerate(pieces)
    ]
    for load in loads:
        load.start()

    def stores(i):
        head = where_ref[0] if heads[i] == 0 else 1 - where_ref[0]
        row = pl.multiple_of(where_ref[1 + i] * 288, 288)
        for h in range(2):
            copy = pltpu.make_async_copy(
                wide.at[i], outs[h].at[pl.ds(row, 288), :], out_sems.at[i]
            )
            yield head == h, copy

    for i in range(count):
        loads[i].wait()
        wide[i] = narrow[i].astype(F32)
        for here, copy in stores(i):
            pl.when(here)(copy.start)
    for i in range(count):
        for here, copy in stores(i):
            pl.when(here)(copy.wait)


def place(where, heads, pieces, held):
    count = len(pieces)
    hbm = pl.BlockSpec(memory_space=pl.ANY)
    return pl.pallas_call(
        functools.partial(place_kernel, heads),
        out_shape=[jax.ShapeDtypeStruct((WIDE, WIDE), F32)] * 2,
        in_specs=[pl.BlockSpec(memory_space=pltpu.SMEM)] + [hbm] * (count + len(held)),
        out_specs=[hbm] * 2,
        input_output_aliases={1 + count + i: i for i in range(len(held))},
        scratch_shapes=[
            pltpu.VMEM((count, 288, WIDE), BF16),
            pltpu.VMEM((count, 288, WIDE), F32),
            pltpu.SemaphoreType.DMA((count,)),
            pltpu.SemaphoreType.DMA((count,)),
        ],
        compiler_params=pltpu.CompilerParams(vmem_limit_bytes=32 * 1024 * 1024),
        name="place",
    )(where, *pieces, *held)


def added(total, parts):
    for part in parts:
        total = total + part.astype(F32)
    return total


def scattered(value, by_route, mine):
    rows = value.shape[0] // 4
    total = lax.dynamic_slice_in_dim(value, mine * rows, rows, 0)
    parts = []
    for by in (1, 3, 2):
        part = lax.dynamic_slice_in_dim(value, lax.rem(mine + by, 4) * rows, rows, 0)
        parts.append(send(part, by_route(by)))
    return added(total, parts)


def local(image_embed, text_embed, image_head, text_head, pair_ids, logit_scale, logit_bias):
    first = lax.axis_index("c") == 0
    scale = logit_scale[0]
    half = scale * (0.5 / math.sqrt(16384))
    knobs = jnp.stack([scale * 0.5, logit_bias[0] * 0.5, half])

    ids_row = jnp.concatenate(
        [(pair_ids // 64).astype(BF16), (pair_ids % 64).astype(BF16), jnp.zeros((896,), BF16)]
    )[None]
    ids_rows = jnp.concatenate([ids_row, jnp.zeros((15, WIDE), BF16)], axis=0)
    mine = jnp.concatenate([jnp.where(first, image_embed, text_embed), ids_rows], axis=0)
    theirs = jnp.concatenate([jnp.where(first, text_embed, image_embed), ids_rows], axis=0)
    heads = (jnp.where(first, image_head, text_head), jnp.where(first, text_head, image_head))

    got = [send(mine, z_pair(0)), send(theirs, z_pair(1))]
    mine, theirs = [
        jnp.concatenate([block[:128], other[:128], block[128:], other[128:]], axis=0)
        for block, other in zip((mine, theirs), got)
    ]
    blocks = [(mine, theirs)]
    for by in (1, 3, 2):
        blocks.append((send(mine, ring(by, 0)), send(theirs, ring(by, 1))))
    own, over, own_rows = [], [], []

    def take(turn):
        message, rows = project(*blocks[turn], heads)
        own.append(message)
        over.append(send(message, other_core))
        own_rows.append(rows)

    for turn in range(3):
        take(turn)
    early = early_pairs(knobs, own, over)
    blocks[3], early = lax.optimization_barrier((blocks[3], early))
    take(3)

    at_x = lax.axis_index("x")
    at_y = lax.axis_index("y")
    at_first = jnp.where(first, at_x, at_y)
    at_second = jnp.where(first, at_y, at_x)
    part, *away = late_pairs(at_first[None], knobs, early, own, over, own_rows)
    part = added(part, [send(piece, ring(by, 0)) for by, piece in zip((1, 3, 2), away)])
    part = scattered(part, lambda by: ring(by, 1), at_second)
    moved = [send(part, z_ring(by)) for by in (1, 3, 2)]
    at_z = lax.axis_index("zh") * 2 + lax.axis_index("zl")
    stack = jnp.zeros((4,) + part.shape, F32)
    for by, piece in zip((0, 1, 3, 2), [part] + moved):
        stack = lax.dynamic_update_slice_in_dim(stack, piece[None], lax.rem(at_z + 4 - by, 4), 0)
    part = ((stack[0] + stack[1]) + (stack[2] + stack[3])).astype(BF16)

    quarter = jnp.zeros((288, WIDE), BF16)
    for by in (0, 1, 3, 2):
        piece = part if by == 0 else send(part, ring(by, 1))
        quarter = lax.dynamic_update_slice_in_dim(
            quarter, piece, lax.rem(at_second + 4 - by, 4) * 72, 0
        )
    core = lax.axis_index("c")

    def where(bys):
        places = [lax.rem(at + 4 - by, 4) for at in (at_first, at_second) for by in bys]
        return jnp.stack([core] + places).astype(jnp.int32)

    pieces = [quarter] + [send(quarter, ring(by, 0)) for by in (1, 3, 2)]
    pieces = pieces + [send(piece, other_core) for piece in pieces]
    places = [lax.rem(at + 4 - by, 4) for at in (at_first, at_second) for by in (0, 1, 3, 2)]
    where = jnp.stack([lax.axis_index("c")] + places).astype(jnp.int32)
    return tuple(place(where, (0, 0, 0, 0, 1, 1, 1, 1), pieces, ()))


def solution(mesh):
    split = Mesh(mesh.devices.reshape(SIZES), AXES)
    every = P(AXES)
    return jax.shard_map(
        local,
        mesh=split,
        in_specs=(every, every, P(), P(), every, P(), P()),
        out_specs=(P(), P()),
        check_vma=False,
    )
```

```python
import functools
import math

import jax
import jax.numpy as jnp
from jax import lax
from jax.experimental import pallas as pl
from jax.experimental.pallas import tpu as pltpu
from jax.sharding import Mesh, PartitionSpec as P

AXES = ("zl", "y", "c", "x", "zh")
SIZES = (2, 4, 2, 4, 2)
BF16 = jnp.bfloat16
F32 = jnp.float32
WIDE = 1152
ROWS = 2048
VMEM_BYTES = 60 * 1024 * 1024


def routes(move):
    pairs = []
    index = 0
    for zl in range(2):
        for y in range(4):
            for c in range(2):
                for x in range(4):
                    for zh in range(2):
                        tzl, ty, tc, tx, tzh = move(zl, y, c, x, zh)
                        pairs.append((index, (((tzl * 4 + ty) * 2 + tc) * 4 + tx) * 2 + tzh))
                        index += 1
    return pairs


def send(value, move):
    return lax.ppermute(value, AXES, routes(move))


def other_core(zl, y, c, x, zh):
    return (zl, y, 1 - c, x, zh)


def z_pair(swap):
    def move(zl, y, c, x, zh):
        return (1 - zl, y, c, x, zh if (c ^ swap) == 0 else 1 - zh)

    return move


def ring(by, swap):
    def move(zl, y, c, x, zh):
        if (c ^ swap) == 0:
            return (zl, y, c, (x + by) % 4, zh)
        return (zl, (y + by) % 4, c, x, zh)

    return move


def z_ring(by):
    def move(zl, y, c, x, zh):
        z = (zh * 2 + zl + by) % 4
        return (z % 2, y, c, x, z // 2)

    return move


def eye_256():
    return lax.broadcasted_iota(jnp.int32, (256, 256), 0) == lax.broadcasted_iota(
        jnp.int32, (256, 256), 1
    )


def as_column(row):
    return jnp.sum(jnp.where(eye_256(), row, 0.0), axis=1, keepdims=True)


def id_row(coded):
    coded = coded.astype(F32)
    parts = [coded[i : i + 1, :128] * 64.0 + coded[i : i + 1, 128:256] for i in (0, 16)]
    return jnp.concatenate(parts, axis=1)


def project_kernel(near, far, head_near, head_far, message, rows_near):
    sides = ((near, head_near, rows_near, 0, 0), (far, head_far, message, 576, 288))
    for block, head, rows, at, to in sides:
        rows[at : at + 256, :] = block[:256, :]
        projected = jnp.dot(block[:256, :], head[...], preferred_element_type=F32)
        inverse = lax.rsqrt(jnp.sum(projected * projected, axis=1, keepdims=True) + 1e-06)
        message[to : to + 256, :] = (projected * inverse).astype(BF16)
        message[to + 256 : to + 288, :] = block[256:288, :]
        rest = jnp.sum(jnp.where(eye_256(), inverse, 0.0), axis=0, keepdims=True)
        lines = lax.broadcasted_iota(jnp.int32, (16, 256), 0)
        coded = block[256:272, :256].astype(F32)
        for line in (1, 2, 3):
            part = rest.astype(BF16).astype(F32)
            coded = jnp.where(lines == line, part, coded)
            rest = rest - part
        message[to + 256 : to + 272, :256] = coded.astype(BF16)


def project(near, far, heads):
    whole = pl.BlockSpec(memory_space=pltpu.VMEM)
    return pl.pallas_call(
        project_kernel,
        out_shape=[
            jax.ShapeDtypeStruct((832, WIDE), BF16),
            jax.ShapeDtypeStruct((256, WIDE), BF16),
        ],
        in_specs=[whole] * 4,
        out_specs=[whole] * 2,
        compiler_params=pltpu.CompilerParams(vmem_limit_bytes=28 * 1024 * 1024),
        cost_estimate=pl.CostEstimate(
            flops=2 * 512 * WIDE * WIDE, bytes_accessed=8_000_000, transcendentals=0
        ),
        name="project",
    )(near, far, *heads)


def unit_loads(sources, units, ids, unit_sems, id_sems):
    loads = []
    for i, (source, start) in enumerate(sources):
        rows = source.at[pl.ds(start, 256), :]
        coded = source.at[pl.ds(start + 256, 32), pl.ds(0, 256)]
        loads.append(
            (
                pltpu.make_async_copy(rows, units.at[pl.ds(i * 256, 256), :], unit_sems.at[i]),
                pltpu.make_async_copy(coded, ids.at[i], id_sems.at[i]),
            )
        )
    return loads


def pair_coefs(knob_ref, near, column, unit, ids, coef, parts):
    half_scale, half_bias, half = knob_ref[0], knob_ref[1], knob_ref[2]
    for part in parts:
        cosine = lax.dot_general(
            near,
            unit[part * 256 : part * 256 + 256, :],
            (((1,), (1,)), ((), ())),
            preferred_element_type=F32,
        )
        base = jnp.where(column == id_row(ids[part]), -half, half)
        value = jnp.tanh(cosine * half_scale + half_bias) * half + base
        coef[:, pl.ds(part * 256, 256)] = value.astype(BF16)


def chunk_column(ids, step):
    return jnp.concatenate([as_column(id_row(ids[2 * step + i])) for i in range(2)], axis=0)


def chunk_inverse(ids, step):
    parts = []
    for i in range(2):
        coded = ids[2 * step + i].astype(F32)
        parts.append(as_column(coded[1:2] + coded[2:3] + coded[3:4]))
    return jnp.concatenate(parts, axis=0)


def unit_sources(own, over):
    near, far = [], []
    for mine, theirs in zip(own, over):
        near += [(mine, 0), (theirs, 288)]
        far += [(mine, 288), (theirs, 0)]
    return near, far


def early_kernel(knob_ref, *refs):
    near_sources, far_sources = unit_sources(refs[:3], refs[3:6])
    grad, near, near_ids, far, far_ids, coef, sems = refs[6:]
    step = pl.program_id(0)
    near_loads = unit_loads(near_sources, near, near_ids, sems.at[0], sems.at[1])
    far_loads = unit_loads(far_sources, far, far_ids, sems.at[2], sems.at[3])

    @pl.when(step == 0)
    def _():
        for pair in far_loads + near_loads:
            for load in pair:
                load.start()
        for pair in far_loads:
            for load in pair:
                load.wait()

    for i, pair in enumerate(near_loads):

        @pl.when(step == i // 2)
        def _(pair=pair):
            for load in pair:
                load.wait()

    rows = near[pl.ds(pl.multiple_of(step * 512, 512), 512), :]
    pair_coefs(knob_ref, rows, chunk_column(near_ids, step), far, far_ids, coef, range(6))
    grad[...] = jnp.dot(coef[...], far[...], preferred_element_type=F32)


def early_pairs(knobs, own, over):
    return pl.pallas_call(
        early_kernel,
        grid=(3,),
        out_shape=jax.ShapeDtypeStruct((1536, WIDE), F32),
        in_specs=[pl.BlockSpec(memory_space=pltpu.SMEM)]
        + [pl.BlockSpec(memory_space=pl.ANY)] * 6,
        out_specs=pl.BlockSpec((512, WIDE), lambda i: (i, 0)),
        scratch_shapes=[
            pltpu.VMEM((1536, WIDE), BF16),
            pltpu.VMEM((6, 32, 256), BF16),
            pltpu.VMEM((1536, WIDE), BF16),
            pltpu.VMEM((6, 32, 256), BF16),
            pltpu.VMEM((512, 1536), BF16),
            pltpu.SemaphoreType.DMA((4, 6)),
        ],
        compiler_params=pltpu.CompilerParams(
            dimension_semantics=("arbitrary",), vmem_limit_bytes=40 * 1024 * 1024
        ),
        cost_estimate=pl.CostEstimate(
            flops=4 * 1536 * 1536 * WIDE, bytes_accessed=14_000_000, transcendentals=1536 * 1536
        ),
        name="early_pairs",
    )(knobs, *own, *over)


def late_kernel(at_ref, knob_ref, early, *refs):
    own, over, own_rows, outs = refs[:4], refs[4:8], refs[8:12], refs[12:16]
    near, near_ids, far, far_ids, rows, grad, coef, total, sems, more_sems = refs[16:]
    near_sources, far_sources = unit_sources(own, over)
    step = pl.program_id(0)
    near_loads = unit_loads(near_sources, near, near_ids, sems.at[0], sems.at[1])
    far_loads = unit_loads(far_sources, far, far_ids, sems.at[2], sems.at[3])
    for i in range(8):
        source = over[i // 2].at[pl.ds(576, 256), :] if i % 2 else own_rows[i // 2]
        near_loads[i] += (
            pltpu.make_async_copy(source, rows.at[pl.ds(i * 256, 256), :], more_sems.at[0, i]),
        )
    for i in range(3):
        near_loads[2 * i] += (
            pltpu.make_async_copy(
                early.at[pl.ds(512 * i, 512), :], grad.at[i], more_sems.at[1, i]
            ),
        )

    @pl.when(step == 0)
    def _():
        for pair in far_loads[6:] + near_loads[:2]:
            for load in pair:
                load.start()
        for pair in far_loads[6:]:
            for load in pair:
                load.wait()
        total[...] = jnp.zeros_like(total)

    for i, pair in enumerate(near_loads):

        @pl.when(step == i // 2)
        def _(pair=pair):
            for load in pair:
                load.wait()

    @pl.when(step == 0)
    def _():
        for pair in near_loads[2:] + far_loads[:6]:
            for load in pair:
                load.start()

    at = pl.ds(pl.multiple_of(step * 512, 512), 512)
    column = chunk_column(near_ids, step)
    inverse = chunk_inverse(near_ids, step)

    def finish(gradient):
        direction = near[at, :].astype(F32)
        radial = jnp.sum(gradient * direction, axis=1, keepdims=True)
        back = ((gradient - radial * direction) * inverse).astype(BF16)
        total[...] += lax.dot_general(
            rows[at, :], back, (((0,), (0,)), ((), ())), preferred_element_type=F32
        )

    @pl.when(step < 3)
    def _():
        pair_coefs(knob_ref, near[at, :], column, far, far_ids, coef, (6, 7))
        more = jnp.dot(coef[:, 1536:], far[1536:, :], preferred_element_type=F32)
        finish(grad[step] + more)

    @pl.when(step == 3)
    def _():
        for pair in far_loads[:6]:
            for load in pair:
                load.wait()
        pair_coefs(knob_ref, near[at, :], column, far, far_ids, coef, range(8))
        finish(jnp.dot(coef[...], far[...], preferred_element_type=F32))
        for by, out in zip((0, 1, 3, 2), outs):
            place = pl.multiple_of(lax.rem(at_ref[0] + by, 4) * 288, 288)
            out[...] = total[pl.ds(place, 288), :].astype(out.dtype)


def late_pairs(at, knobs, early, own, over, own_rows):
    smem = pl.BlockSpec(memory_space=pltpu.SMEM)
    return pl.pallas_call(
        late_kernel,
        grid=(4,),
        out_shape=[jax.ShapeDtypeStruct((288, WIDE), kind) for kind in (F32, BF16, BF16, BF16)],
        in_specs=[smem, smem] + [pl.BlockSpec(memory_space=pl.ANY)] * 13,
        out_specs=[
            pl.BlockSpec((288, WIDE), lambda i: (0, 0), pipeline_mode=pl.Buffered(1))
        ]
        * 4,
        scratch_shapes=[
            pltpu.VMEM((ROWS, WIDE), BF16),
            pltpu.VMEM((8, 32, 256), BF16),
            pltpu.VMEM((ROWS, WIDE), BF16),
            pltpu.VMEM((8, 32, 256), BF16),
            pltpu.VMEM((ROWS, WIDE), BF16),
            pltpu.VMEM((3, 512, WIDE), F32),
            pltpu.VMEM((512, ROWS), BF16),
            pltpu.VMEM((WIDE, WIDE), F32),
            pltpu.SemaphoreType.DMA((4, 8)),
            pltpu.SemaphoreType.DMA((2, 8)),
        ],
        compiler_params=pltpu.CompilerParams(
            dimension_semantics=("arbitrary",), vmem_limit_bytes=VMEM_BYTES
        ),
        cost_estimate=pl.CostEstimate(
            flops=4 * 7 * 512 * 512 * WIDE + 2 * ROWS * WIDE * WIDE,
            bytes_accessed=25_000_000,
            transcendentals=7 * 512 * 512,
        ),
        name="late_pairs",
    )(at, knobs, early, *own, *over, *own_rows)


def place_kernel(heads, where_ref, *refs):
    count = len(heads)
    pieces, outs = refs[:count], refs[-6:-4]
    narrow, wide, in_sems, out_sems = refs[-4:]
    loads = [
        pltpu.make_async_copy(piece, narrow.at[i], in_sems.at[i]) for i, piece in enumerate(pieces)
    ]
    for load in loads:
        load.start()

    def stores(i):
        head = where_ref[0] if heads[i] == 0 else 1 - where_ref[0]
        row = pl.multiple_of(where_ref[1 + i] * 288, 288)
        for h in range(2):
            copy = pltpu.make_async_copy(
                wide.at[i], outs[h].at[pl.ds(row, 288), :], out_sems.at[i]
            )
            yield head == h, copy

    for i in range(count):
        loads[i].wait()
        wide[i] = narrow[i].astype(F32)
        for here, copy in stores(i):
            pl.when(here)(copy.start)
    for i in range(count):
        for here, copy in stores(i):
            pl.when(here)(copy.wait)


def place(where, heads, pieces, held):
    count = len(pieces)
    hbm = pl.BlockSpec(memory_space=pl.ANY)
    return pl.pallas_call(
        functools.partial(place_kernel, heads),
        out_shape=[jax.ShapeDtypeStruct((WIDE, WIDE), F32)] * 2,
        in_specs=[pl.BlockSpec(memory_space=pltpu.SMEM)] + [hbm] * (count + len(held)),
        out_specs=[hbm] * 2,
        input_output_aliases={1 + count + i: i for i in range(len(held))},
        scratch_shapes=[
            pltpu.VMEM((count, 288, WIDE), BF16),
            pltpu.VMEM((count, 288, WIDE), F32),
            pltpu.SemaphoreType.DMA((count,)),
            pltpu.SemaphoreType.DMA((count,)),
        ],
        compiler_params=pltpu.CompilerParams(vmem_limit_bytes=32 * 1024 * 1024),
        name="place",
    )(where, *pieces, *held)


def added(total, parts):
    for part in parts:
        total = total + part.astype(F32)
    return total


def scattered(value, by_route, mine):
    rows = value.shape[0] // 4
    total = lax.dynamic_slice_in_dim(value, mine * rows, rows, 0)
    parts = []
    for by in (1, 3, 2):
        part = lax.dynamic_slice_in_dim(value, lax.rem(mine + by, 4) * rows, rows, 0)
        parts.append(send(part, by_route(by)))
    return added(total, parts)


def local(image_embed, text_embed, image_head, text_head, pair_ids, logit_scale, logit_bias):
    first = lax.axis_index("c") == 0
    scale = logit_scale[0]
    half = scale * (0.5 / math.sqrt(16384))
    knobs = jnp.stack([scale * 0.5, logit_bias[0] * 0.5, half])

    ids_row = jnp.concatenate(
        [(pair_ids // 64).astype(BF16), (pair_ids % 64).astype(BF16), jnp.zeros((896,), BF16)]
    )[None]
    ids_rows = jnp.concatenate([ids_row, jnp.zeros((15, WIDE), BF16)], axis=0)
    mine = jnp.concatenate([jnp.where(first, image_embed, text_embed), ids_rows], axis=0)
    theirs = jnp.concatenate([jnp.where(first, text_embed, image_embed), ids_rows], axis=0)
    heads = (jnp.where(first, image_head, text_head), jnp.where(first, text_head, image_head))

    got = [send(mine, z_pair(0)), send(theirs, z_pair(1))]
    mine, theirs = [
        jnp.concatenate([block[:128], other[:128], block[128:], other[128:]], axis=0)
        for block, other in zip((mine, theirs), got)
    ]
    blocks = [(mine, theirs)]
    for by in (1, 3, 2):
        blocks.append((send(mine, ring(by, 0)), send(theirs, ring(by, 1))))
    own, over, own_rows = [], [], []

    def take(turn):
        message, rows = project(*blocks[turn], heads)
        own.append(message)
        over.append(send(message, other_core))
        own_rows.append(rows)

    for turn in range(3):
        take(turn)
    early = early_pairs(knobs, own, over)
    blocks[3], early = lax.optimization_barrier((blocks[3], early))
    take(3)

    at_x = lax.axis_index("x")
    at_y = lax.axis_index("y")
    at_first = jnp.where(first, at_x, at_y)
    at_second = jnp.where(first, at_y, at_x)
    part, *away = late_pairs(at_first[None], knobs, early, own, over, own_rows)
    part = added(part, [send(piece, ring(by, 0)) for by, piece in zip((1, 3, 2), away)])
    part = scattered(part, lambda by: ring(by, 1), at_second)
    moved = [send(part, z_ring(by)) for by in (1, 3, 2)]
    at_z = lax.axis_index("zh") * 2 + lax.axis_index("zl")
    stack = jnp.zeros((4,) + part.shape, F32)
    for by, piece in zip((0, 1, 3, 2), [part] + moved):
        stack = lax.dynamic_update_slice_in_dim(stack, piece[None], lax.rem(at_z + 4 - by, 4), 0)
    part = ((stack[0] + stack[1]) + (stack[2] + stack[3])).astype(BF16)

    quarter = jnp.zeros((288, WIDE), BF16)
    for by in (0, 1, 3, 2):
        piece = part if by == 0 else send(part, ring(by, 1))
        quarter = lax.dynamic_update_slice_in_dim(
            quarter, piece, lax.rem(at_second + 4 - by, 4) * 72, 0
        )
    core = lax.axis_index("c")

    def where(bys):
        places = [lax.rem(at + 4 - by, 4) for at in (at_first, at_second) for by in bys]
        return jnp.stack([core] + places).astype(jnp.int32)

    pieces = [quarter] + [send(quarter, ring(by, 0)) for by in (1, 3, 2)]
    pieces = pieces + [send(piece, other_core) for piece in pieces]
    places = [lax.rem(at + 4 - by, 4) for at in (at_first, at_second) for by in (0, 1, 3, 2)]
    where = jnp.stack([lax.axis_index("c")] + places).astype(jnp.int32)
    return tuple(place(where, (0, 0, 0, 0, 1, 1, 1, 1), pieces, ()))


def solution(mesh):
    split = Mesh(mesh.devices.reshape(SIZES), AXES)
    every = P(AXES)
    return jax.shard_map(
        local,
        mesh=split,
        in_specs=(every, every, P(), P(), every, P(), P()),
        out_specs=(P(), P()),
        check_vma=False,
    )
```

```python
import functools
import math

import jax
import jax.numpy as jnp
from jax import lax
from jax.experimental import pallas as pl
from jax.experimental.pallas import tpu as pltpu
from jax.sharding import Mesh, PartitionSpec as P

AXES = ("zl", "y", "c", "x", "zh")
SIZES = (2, 4, 2, 4, 2)
BF16 = jnp.bfloat16
F32 = jnp.float32
WIDE = 1152
ROWS = 2048
VMEM_BYTES = 60 * 1024 * 1024


def routes(move):
    pairs = []
    index = 0
    for zl in range(2):
        for y in range(4):
            for c in range(2):
                for x in range(4):
                    for zh in range(2):
                        tzl, ty, tc, tx, tzh = move(zl, y, c, x, zh)
                        pairs.append((index, (((tzl * 4 + ty) * 2 + tc) * 4 + tx) * 2 + tzh))
                        index += 1
    return pairs


def send(value, move):
    return lax.ppermute(value, AXES, routes(move))


def other_core(zl, y, c, x, zh):
    return (zl, y, 1 - c, x, zh)


def z_pair(swap):
    def move(zl, y, c, x, zh):
        return (1 - zl, y, c, x, zh if (c ^ swap) == 0 else 1 - zh)

    return move


def ring(by, swap):
    def move(zl, y, c, x, zh):
        if (c ^ swap) == 0:
            return (zl, y, c, (x + by) % 4, zh)
        return (zl, (y + by) % 4, c, x, zh)

    return move


def z_ring(by):
    def move(zl, y, c, x, zh):
        z = (zh * 2 + zl + by) % 4
        return (z % 2, y, c, x, z // 2)

    return move


def eye_256():
    return lax.broadcasted_iota(jnp.int32, (256, 256), 0) == lax.broadcasted_iota(
        jnp.int32, (256, 256), 1
    )


def as_column(row):
    return jnp.sum(jnp.where(eye_256(), row, 0.0), axis=1, keepdims=True)


def id_row(coded):
    coded = coded.astype(F32)
    parts = [coded[i : i + 1, :128] * 64.0 + coded[i : i + 1, 128:256] for i in (0, 16)]
    return jnp.concatenate(parts, axis=1)


def project_kernel(near, far, head_near, head_far, message, rows_near):
    sides = ((near, head_near, rows_near, 0, 0), (far, head_far, message, 576, 288))
    for block, head, rows, at, to in sides:
        rows[at : at + 256, :] = block[:256, :]
        projected = jnp.dot(block[:256, :], head[...], preferred_element_type=F32)
        inverse = lax.rsqrt(jnp.sum(projected * projected, axis=1, keepdims=True) + 1e-06)
        message[to : to + 256, :] = (projected * inverse).astype(BF16)
        message[to + 256 : to + 288, :] = block[256:288, :]
        rest = jnp.sum(jnp.where(eye_256(), inverse, 0.0), axis=0, keepdims=True)
        lines = lax.broadcasted_iota(jnp.int32, (16, 256), 0)
        coded = block[256:272, :256].astype(F32)
        for line in (1, 2, 3):
            part = rest.astype(BF16).astype(F32)
            coded = jnp.where(lines == line, part, coded)
            rest = rest - part
        message[to + 256 : to + 272, :256] = coded.astype(BF16)


def project(near, far, heads):
    whole = pl.BlockSpec(memory_space=pltpu.VMEM)
    return pl.pallas_call(
        project_kernel,
        out_shape=[
            jax.ShapeDtypeStruct((832, WIDE), BF16),
            jax.ShapeDtypeStruct((256, WIDE), BF16),
        ],
        in_specs=[whole] * 4,
        out_specs=[whole] * 2,
        compiler_params=pltpu.CompilerParams(vmem_limit_bytes=28 * 1024 * 1024),
        cost_estimate=pl.CostEstimate(
            flops=2 * 512 * WIDE * WIDE, bytes_accessed=8_000_000, transcendentals=0
        ),
        name="project",
    )(near, far, *heads)


def unit_loads(sources, units, ids, unit_sems, id_sems):
    loads = []
    for i, (source, start) in enumerate(sources):
        rows = source.at[pl.ds(start, 256), :]
        coded = source.at[pl.ds(start + 256, 32), pl.ds(0, 256)]
        loads.append(
            (
                pltpu.make_async_copy(rows, units.at[pl.ds(i * 256, 256), :], unit_sems.at[i]),
                pltpu.make_async_copy(coded, ids.at[i], id_sems.at[i]),
            )
        )
    return loads


def pair_coefs(knob_ref, near, column, unit, ids, coef, parts):
    half_scale, half_bias, half = knob_ref[0], knob_ref[1], knob_ref[2]
    for part in parts:
        cosine = lax.dot_general(
            near,
            unit[part * 256 : part * 256 + 256, :],
            (((1,), (1,)), ((), ())),
            preferred_element_type=F32,
        )
        base = jnp.where(column == id_row(ids[part]), -half, half)
        value = jnp.tanh(cosine * half_scale + half_bias) * half + base
        coef[:, pl.ds(part * 256, 256)] = value.astype(BF16)


def chunk_column(ids, step):
    return jnp.concatenate([as_column(id_row(ids[2 * step + i])) for i in range(2)], axis=0)


def chunk_inverse(ids, step):
    parts = []
    for i in range(2):
        coded = ids[2 * step + i].astype(F32)
        parts.append(as_column(coded[1:2] + coded[2:3] + coded[3:4]))
    return jnp.concatenate(parts, axis=0)


def unit_sources(own, over):
    near, far = [], []
    for mine, theirs in zip(own, over):
        near += [(mine, 0), (theirs, 288)]
        far += [(mine, 288), (theirs, 0)]
    return near, far


def early_kernel(knob_ref, *refs):
    near_sources, far_sources = unit_sources(refs[:3], refs[3:6])
    grad, near, near_ids, far, far_ids, coef, sems = refs[6:]
    step = pl.program_id(0)
    near_loads = unit_loads(near_sources, near, near_ids, sems.at[0], sems.at[1])
    far_loads = unit_loads(far_sources, far, far_ids, sems.at[2], sems.at[3])

    @pl.when(step == 0)
    def _():
        for pair in far_loads + near_loads:
            for load in pair:
                load.start()
        for pair in far_loads:
            for load in pair:
                load.wait()

    for i, pair in enumerate(near_loads):

        @pl.when(step == i // 2)
        def _(pair=pair):
            for load in pair:
                load.wait()

    rows = near[pl.ds(pl.multiple_of(step * 512, 512), 512), :]
    pair_coefs(knob_ref, rows, chunk_column(near_ids, step), far, far_ids, coef, range(6))
    grad[...] = jnp.dot(coef[...], far[...], preferred_element_type=F32)


def early_pairs(knobs, own, over):
    return pl.pallas_call(
        early_kernel,
        grid=(3,),
        out_shape=jax.ShapeDtypeStruct((1536, WIDE), F32),
        in_specs=[pl.BlockSpec(memory_space=pltpu.SMEM)]
        + [pl.BlockSpec(memory_space=pl.ANY)] * 6,
        out_specs=pl.BlockSpec((512, WIDE), lambda i: (i, 0)),
        scratch_shapes=[
            pltpu.VMEM((1536, WIDE), BF16),
            pltpu.VMEM((6, 32, 256), BF16),
            pltpu.VMEM((1536, WIDE), BF16),
            pltpu.VMEM((6, 32, 256), BF16),
            pltpu.VMEM((512, 1536), BF16),
            pltpu.SemaphoreType.DMA((4, 6)),
        ],
        compiler_params=pltpu.CompilerParams(
            dimension_semantics=("arbitrary",), vmem_limit_bytes=40 * 1024 * 1024
        ),
        cost_estimate=pl.CostEstimate(
            flops=4 * 1536 * 1536 * WIDE, bytes_accessed=14_000_000, transcendentals=1536 * 1536
        ),
        name="early_pairs",
    )(knobs, *own, *over)


def late_kernel(at_ref, knob_ref, early, *refs):
    own, over, own_rows, outs = refs[:4], refs[4:8], refs[8:12], refs[12:16]
    near, near_ids, far, far_ids, rows, grad, coef, total, sems, more_sems = refs[16:]
    near_sources, far_sources = unit_sources(own, over)
    step = pl.program_id(0)
    near_loads = unit_loads(near_sources, near, near_ids, sems.at[0], sems.at[1])
    far_loads = unit_loads(far_sources, far, far_ids, sems.at[2], sems.at[3])
    for i in range(8):
        source = over[i // 2].at[pl.ds(576, 256), :] if i % 2 else own_rows[i // 2]
        near_loads[i] += (
            pltpu.make_async_copy(source, rows.at[pl.ds(i * 256, 256), :], more_sems.at[0, i]),
        )
    for i in range(3):
        near_loads[2 * i] += (
            pltpu.make_async_copy(
                early.at[pl.ds(512 * i, 512), :], grad.at[i], more_sems.at[1, i]
            ),
        )

    @pl.when(step == 0)
    def _():
        for pair in far_loads[6:] + near_loads[:2]:
            for load in pair:
                load.start()
        for pair in far_loads[6:]:
            for load in pair:
                load.wait()
        total[...] = jnp.zeros_like(total)

    for i, pair in enumerate(near_loads):

        @pl.when(step == i // 2)
        def _(pair=pair):
            for load in pair:
                load.wait()

    @pl.when(step == 0)
    def _():
        for pair in near_loads[2:] + far_loads[:6]:
            for load in pair:
                load.start()

    at = pl.ds(pl.multiple_of(step * 512, 512), 512)
    column = chunk_column(near_ids, step)
    inverse = chunk_inverse(near_ids, step)

    def finish(gradient):
        direction = near[at, :].astype(F32)
        radial = jnp.sum(gradient * direction, axis=1, keepdims=True)
        back = ((gradient - radial * direction) * inverse).astype(BF16)
        total[...] += lax.dot_general(
            rows[at, :], back, (((0,), (0,)), ((), ())), preferred_element_type=F32
        )

    @pl.when(step < 3)
    def _():
        pair_coefs(knob_ref, near[at, :], column, far, far_ids, coef, (6, 7))
        more = jnp.dot(coef[:, 1536:], far[1536:, :], preferred_element_type=F32)
        finish(grad[step] + more)

    @pl.when(step == 3)
    def _():
        for pair in far_loads[:6]:
            for load in pair:
                load.wait()
        pair_coefs(knob_ref, near[at, :], column, far, far_ids, coef, range(8))
        finish(jnp.dot(coef[...], far[...], preferred_element_type=F32))
        for by, out in zip((0, 1, 3, 2), outs):
            place = pl.multiple_of(lax.rem(at_ref[0] + by, 4) * 288, 288)
            out[...] = total[pl.ds(place, 288), :].astype(out.dtype)


def late_pairs(at, knobs, early, own, over, own_rows):
    smem = pl.BlockSpec(memory_space=pltpu.SMEM)
    return pl.pallas_call(
        late_kernel,
        grid=(4,),
        out_shape=[jax.ShapeDtypeStruct((288, WIDE), kind) for kind in (F32, BF16, BF16, BF16)],
        in_specs=[smem, smem] + [pl.BlockSpec(memory_space=pl.ANY)] * 13,
        out_specs=[
            pl.BlockSpec((288, WIDE), lambda i: (0, 0), pipeline_mode=pl.Buffered(1))
        ]
        * 4,
        scratch_shapes=[
            pltpu.VMEM((ROWS, WIDE), BF16),
            pltpu.VMEM((8, 32, 256), BF16),
            pltpu.VMEM((ROWS, WIDE), BF16),
            pltpu.VMEM((8, 32, 256), BF16),
            pltpu.VMEM((ROWS, WIDE), BF16),
            pltpu.VMEM((3, 512, WIDE), F32),
            pltpu.VMEM((512, ROWS), BF16),
            pltpu.VMEM((WIDE, WIDE), F32),
            pltpu.SemaphoreType.DMA((4, 8)),
            pltpu.SemaphoreType.DMA((2, 8)),
        ],
        compiler_params=pltpu.CompilerParams(
            dimension_semantics=("arbitrary",), vmem_limit_bytes=VMEM_BYTES
        ),
        cost_estimate=pl.CostEstimate(
            flops=4 * 7 * 512 * 512 * WIDE + 2 * ROWS * WIDE * WIDE,
            bytes_accessed=25_000_000,
            transcendentals=7 * 512 * 512,
        ),
        name="late_pairs",
    )(at, knobs, early, *own, *over, *own_rows)


def place_kernel(*refs):
    pieces, outs = refs[:8], refs[8:10]
    wide, sems = refs[10:]
    core, at_x, at_y = (lax.axis_index(axis) for axis in ("c", "x", "y"))

    def stores(i):
        mine = i < 4
        head = core if mine else 1 - core
        at = jnp.where(head == 0, at_x, at_y)
        row = pl.multiple_of(lax.rem(at + 4 - (0, 1, 3, 2)[i % 4], 4) * 288, 288)
        for h in range(2):
            copy = pltpu.make_async_copy(wide.at[i], outs[h].at[pl.ds(row, 288), :], sems.at[i])
            yield head == h, copy

    for i in (0, 4, 1, 5, 2, 6, 3, 7):
        wide[i] = pieces[i][...].astype(F32)
        for here, copy in stores(i):
            pl.when(here)(copy.start)
    for i in range(8):
        for here, copy in stores(i):
            pl.when(here)(copy.wait)


def place(pieces):
    anywhere = pl.BlockSpec(memory_space=pl.ANY)
    return pl.pallas_call(
        place_kernel,
        out_shape=[jax.ShapeDtypeStruct((WIDE, WIDE), F32)] * 2,
        in_specs=[pl.BlockSpec(memory_space=pltpu.VMEM)] * 8,
        out_specs=[anywhere] * 2,
        scratch_shapes=[pltpu.VMEM((8, 288, WIDE), F32), pltpu.SemaphoreType.DMA((8,))],
        compiler_params=pltpu.CompilerParams(vmem_limit_bytes=16 * 1024 * 1024),
        name="place",
    )(*pieces)


def added(total, parts):
    for part in parts:
        total = total + part.astype(F32)
    return total


def scattered(value, by_route, mine):
    rows = value.shape[0] // 4
    total = lax.dynamic_slice_in_dim(value, mine * rows, rows, 0)
    parts = []
    for by in (1, 3, 2):
        part = lax.dynamic_slice_in_dim(value, lax.rem(mine + by, 4) * rows, rows, 0)
        parts.append(send(part, by_route(by)))
    return added(total, parts)


def local(image_embed, text_embed, image_head, text_head, pair_ids, logit_scale, logit_bias):
    first = lax.axis_index("c") == 0
    scale = logit_scale[0]
    half = scale * (0.5 / math.sqrt(16384))
    knobs = jnp.stack([scale * 0.5, logit_bias[0] * 0.5, half])

    ids_row = jnp.concatenate(
        [(pair_ids // 64).astype(BF16), (pair_ids % 64).astype(BF16), jnp.zeros((896,), BF16)]
    )[None]
    ids_rows = jnp.concatenate([ids_row, jnp.zeros((15, WIDE), BF16)], axis=0)
    mine = jnp.concatenate([jnp.where(first, image_embed, text_embed), ids_rows], axis=0)
    theirs = jnp.concatenate([jnp.where(first, text_embed, image_embed), ids_rows], axis=0)
    heads = (jnp.where(first, image_head, text_head), jnp.where(first, text_head, image_head))

    got = [send(mine, z_pair(0)), send(theirs, z_pair(1))]
    mine, theirs = [
        jnp.concatenate([block[:128], other[:128], block[128:], other[128:]], axis=0)
        for block, other in zip((mine, theirs), got)
    ]
    blocks = [(mine, theirs)]
    for by in (1, 3, 2):
        blocks.append((send(mine, ring(by, 0)), send(theirs, ring(by, 1))))
    own, over, own_rows = [], [], []

    def take(turn):
        message, rows = project(*blocks[turn], heads)
        own.append(message)
        over.append(send(message, other_core))
        own_rows.append(rows)

    for turn in range(3):
        take(turn)
    early = early_pairs(knobs, own, over)
    blocks[3], early = lax.optimization_barrier((blocks[3], early))
    take(3)

    at_x = lax.axis_index("x")
    at_y = lax.axis_index("y")
    at_first = jnp.where(first, at_x, at_y)
    at_second = jnp.where(first, at_y, at_x)
    part, *away = late_pairs(at_first[None], knobs, early, own, over, own_rows)
    part = added(part, [send(piece, ring(by, 0)) for by, piece in zip((1, 3, 2), away)])
    part = scattered(part, lambda by: ring(by, 1), at_second)
    moved = [send(part, z_ring(by)) for by in (1, 3, 2)]
    at_z = lax.axis_index("zh") * 2 + lax.axis_index("zl")
    stack = jnp.zeros((4,) + part.shape, F32)
    for by, piece in zip((0, 1, 3, 2), [part] + moved):
        stack = lax.dynamic_update_slice_in_dim(stack, piece[None], lax.rem(at_z + 4 - by, 4), 0)
    part = ((stack[0] + stack[1]) + (stack[2] + stack[3])).astype(BF16)

    quarter = jnp.zeros((288, WIDE), BF16)
    for by in (0, 1, 3, 2):
        piece = part if by == 0 else send(part, ring(by, 1))
        quarter = lax.dynamic_update_slice_in_dim(
            quarter, piece, lax.rem(at_second + 4 - by, 4) * 72, 0
        )
    pieces = [quarter] + [send(quarter, ring(by, 0)) for by in (1, 3, 2)]
    pieces = pieces + [send(piece, other_core) for piece in pieces]
    return tuple(place(pieces))


def solution(mesh):
    split = Mesh(mesh.devices.reshape(SIZES), AXES)
    every = P(AXES)
    return jax.shard_map(
        local,
        mesh=split,
        in_specs=(every, every, P(), P(), every, P(), P()),
        out_specs=(P(), P()),
        check_vma=False,
    )
```

```python
import functools
import math

import jax
import jax.numpy as jnp
from jax import lax
from jax.experimental import pallas as pl
from jax.experimental.pallas import tpu as pltpu
from jax.sharding import Mesh, PartitionSpec as P

AXES = ("zl", "y", "c", "x", "zh")
SIZES = (2, 4, 2, 4, 2)
BF16 = jnp.bfloat16
F32 = jnp.float32
WIDE = 1152
ROWS = 2048
VMEM_BYTES = 60 * 1024 * 1024


def routes(move):
    pairs = []
    index = 0
    for zl in range(2):
        for y in range(4):
            for c in range(2):
                for x in range(4):
                    for zh in range(2):
                        tzl, ty, tc, tx, tzh = move(zl, y, c, x, zh)
                        pairs.append((index, (((tzl * 4 + ty) * 2 + tc) * 4 + tx) * 2 + tzh))
                        index += 1
    return pairs


def send(value, move):
    return lax.ppermute(value, AXES, routes(move))


def other_core(zl, y, c, x, zh):
    return (zl, y, 1 - c, x, zh)


def z_pair(swap):
    def move(zl, y, c, x, zh):
        return (1 - zl, y, c, x, zh if (c ^ swap) == 0 else 1 - zh)

    return move


def ring(by, swap):
    def move(zl, y, c, x, zh):
        if (c ^ swap) == 0:
            return (zl, y, c, (x + by) % 4, zh)
        return (zl, (y + by) % 4, c, x, zh)

    return move


def z_ring(by):
    def move(zl, y, c, x, zh):
        z = (zh * 2 + zl + by) % 4
        return (z % 2, y, c, x, z // 2)

    return move


def eye_256():
    return lax.broadcasted_iota(jnp.int32, (256, 256), 0) == lax.broadcasted_iota(
        jnp.int32, (256, 256), 1
    )


def as_column(row):
    return jnp.sum(jnp.where(eye_256(), row, 0.0), axis=1, keepdims=True)


def id_row(coded):
    coded = coded.astype(F32)
    parts = [coded[i : i + 1, :128] * 64.0 + coded[i : i + 1, 128:256] for i in (0, 1)]
    return jnp.concatenate(parts, axis=1)


def project_kernel(near, far, head_near, head_far, message, rows_near):
    sides = ((near, head_near, rows_near, 0, 0), (far, head_far, message, 544, 272))
    for block, head, rows, at, to in sides:
        rows[at : at + 256, :] = block[:256, :]
        projected = jnp.dot(block[:256, :], head[...], preferred_element_type=F32)
        inverse = lax.rsqrt(jnp.sum(projected * projected, axis=1, keepdims=True) + 1e-06)
        message[to : to + 256, :] = (projected * inverse).astype(BF16)
        message[to + 256 : to + 272, :] = block[256:272, :]
        rest = jnp.sum(jnp.where(eye_256(), inverse, 0.0), axis=0, keepdims=True)
        lines = lax.broadcasted_iota(jnp.int32, (16, 256), 0)
        coded = block[256:272, :256].astype(F32)
        for line in (2, 3, 4):
            part = rest.astype(BF16).astype(F32)
            coded = jnp.where(lines == line, part, coded)
            rest = rest - part
        message[to + 256 : to + 272, :256] = coded.astype(BF16)


def project(near, far, heads):
    whole = pl.BlockSpec(memory_space=pltpu.VMEM)
    return pl.pallas_call(
        project_kernel,
        out_shape=[
            jax.ShapeDtypeStruct((800, WIDE), BF16),
            jax.ShapeDtypeStruct((256, WIDE), BF16),
        ],
        in_specs=[whole] * 4,
        out_specs=[whole] * 2,
        compiler_params=pltpu.CompilerParams(vmem_limit_bytes=28 * 1024 * 1024),
        cost_estimate=pl.CostEstimate(
            flops=2 * 512 * WIDE * WIDE, bytes_accessed=8_000_000, transcendentals=0
        ),
        name="project",
    )(near, far, *heads)


def unit_loads(sources, units, ids, unit_sems, id_sems):
    loads = []
    for i, (source, start) in enumerate(sources):
        rows = source.at[pl.ds(start, 256), :]
        coded = source.at[pl.ds(start + 256, 16), pl.ds(0, 256)]
        loads.append(
            (
                pltpu.make_async_copy(rows, units.at[pl.ds(i * 256, 256), :], unit_sems.at[i]),
                pltpu.make_async_copy(coded, ids.at[i], id_sems.at[i]),
            )
        )
    return loads


def pair_coefs(knob_ref, near, column, unit, ids, coef, parts):
    half_scale, half_bias, half = knob_ref[0], knob_ref[1], knob_ref[2]
    for part in parts:
        cosine = lax.dot_general(
            near,
            unit[part * 256 : part * 256 + 256, :],
            (((1,), (1,)), ((), ())),
            preferred_element_type=F32,
        )
        base = jnp.where(column == id_row(ids[part]), -half, half)
        value = jnp.tanh(cosine * half_scale + half_bias) * half + base
        coef[:, pl.ds(part * 256, 256)] = value.astype(BF16)


def chunk_column(ids, step):
    return jnp.concatenate([as_column(id_row(ids[2 * step + i])) for i in range(2)], axis=0)


def chunk_inverse(ids, step):
    parts = []
    for i in range(2):
        coded = ids[2 * step + i].astype(F32)
        parts.append(as_column(coded[2:3] + coded[3:4] + coded[4:5]))
    return jnp.concatenate(parts, axis=0)


def unit_sources(own, over):
    near, far = [], []
    for mine, theirs in zip(own, over):
        near += [(mine, 0), (theirs, 272)]
        far += [(mine, 272), (theirs, 0)]
    return near, far


def early_kernel(knob_ref, *refs):
    near_sources, far_sources = unit_sources(refs[:3], refs[3:6])
    grad, near, near_ids, far, far_ids, coef, sems = refs[6:]
    step = pl.program_id(0)
    near_loads = unit_loads(near_sources, near, near_ids, sems.at[0], sems.at[1])
    far_loads = unit_loads(far_sources, far, far_ids, sems.at[2], sems.at[3])

    @pl.when(step == 0)
    def _():
        for pair in far_loads + near_loads:
            for load in pair:
                load.start()
        for pair in far_loads:
            for load in pair:
                load.wait()

    for i, pair in enumerate(near_loads):

        @pl.when(step == i // 2)
        def _(pair=pair):
            for load in pair:
                load.wait()

    rows = near[pl.ds(pl.multiple_of(step * 512, 512), 512), :]
    pair_coefs(knob_ref, rows, chunk_column(near_ids, step), far, far_ids, coef, range(6))
    grad[...] = jnp.dot(coef[...], far[...], preferred_element_type=F32)


def early_pairs(knobs, own, over):
    return pl.pallas_call(
        early_kernel,
        grid=(3,),
        out_shape=jax.ShapeDtypeStruct((1536, WIDE), F32),
        in_specs=[pl.BlockSpec(memory_space=pltpu.SMEM)]
        + [pl.BlockSpec(memory_space=pl.ANY)] * 6,
        out_specs=pl.BlockSpec((512, WIDE), lambda i: (i, 0)),
        scratch_shapes=[
            pltpu.VMEM((1536, WIDE), BF16),
            pltpu.VMEM((6, 16, 256), BF16),
            pltpu.VMEM((1536, WIDE), BF16),
            pltpu.VMEM((6, 16, 256), BF16),
            pltpu.VMEM((512, 1536), BF16),
            pltpu.SemaphoreType.DMA((4, 6)),
        ],
        compiler_params=pltpu.CompilerParams(
            dimension_semantics=("arbitrary",), vmem_limit_bytes=40 * 1024 * 1024
        ),
        cost_estimate=pl.CostEstimate(
            flops=4 * 1536 * 1536 * WIDE, bytes_accessed=14_000_000, transcendentals=1536 * 1536
        ),
        name="early_pairs",
    )(knobs, *own, *over)


def late_kernel(at_ref, knob_ref, early, *refs):
    own, over, own_rows, outs = refs[:4], refs[4:8], refs[8:12], refs[12:16]
    near, near_ids, far, far_ids, rows, grad, coef, total, sems, more_sems = refs[16:]
    near_sources, far_sources = unit_sources(own, over)
    step = pl.program_id(0)
    near_loads = unit_loads(near_sources, near, near_ids, sems.at[0], sems.at[1])
    far_loads = unit_loads(far_sources, far, far_ids, sems.at[2], sems.at[3])
    for i in range(8):
        source = over[i // 2].at[pl.ds(544, 256), :] if i % 2 else own_rows[i // 2]
        near_loads[i] += (
            pltpu.make_async_copy(source, rows.at[pl.ds(i * 256, 256), :], more_sems.at[0, i]),
        )
    for i in range(3):
        near_loads[2 * i] += (
            pltpu.make_async_copy(
                early.at[pl.ds(512 * i, 512), :], grad.at[i], more_sems.at[1, i]
            ),
        )

    @pl.when(step == 0)
    def _():
        for pair in far_loads[6:] + near_loads[:2]:
            for load in pair:
                load.start()
        for pair in far_loads[6:]:
            for load in pair:
                load.wait()
        total[...] = jnp.zeros_like(total)

    for i, pair in enumerate(near_loads):

        @pl.when(step == i // 2)
        def _(pair=pair):
            for load in pair:
                load.wait()

    @pl.when(step == 0)
    def _():
        for pair in near_loads[2:] + far_loads[:6]:
            for load in pair:
                load.start()

    at = pl.ds(pl.multiple_of(step * 512, 512), 512)
    column = chunk_column(near_ids, step)
    inverse = chunk_inverse(near_ids, step)

    def finish(gradient):
        direction = near[at, :].astype(F32)
        radial = jnp.sum(gradient * direction, axis=1, keepdims=True)
        back = ((gradient - radial * direction) * inverse).astype(BF16)
        total[...] += lax.dot_general(
            rows[at, :], back, (((0,), (0,)), ((), ())), preferred_element_type=F32
        )

    @pl.when(step < 3)
    def _():
        pair_coefs(knob_ref, near[at, :], column, far, far_ids, coef, (6, 7))
        more = jnp.dot(coef[:, 1536:], far[1536:, :], preferred_element_type=F32)
        finish(grad[step] + more)

    @pl.when(step == 3)
    def _():
        for pair in far_loads[:6]:
            for load in pair:
                load.wait()
        pair_coefs(knob_ref, near[at, :], column, far, far_ids, coef, range(8))
        finish(jnp.dot(coef[...], far[...], preferred_element_type=F32))
        for by, out in zip((0, 1, 3, 2), outs):
            place = pl.multiple_of(lax.rem(at_ref[0] + by, 4) * 288, 288)
            out[...] = total[pl.ds(place, 288), :].astype(out.dtype)


def late_pairs(at, knobs, early, own, over, own_rows):
    smem = pl.BlockSpec(memory_space=pltpu.SMEM)
    return pl.pallas_call(
        late_kernel,
        grid=(4,),
        out_shape=[jax.ShapeDtypeStruct((288, WIDE), kind) for kind in (F32, BF16, BF16, BF16)],
        in_specs=[smem, smem] + [pl.BlockSpec(memory_space=pl.ANY)] * 13,
        out_specs=[
            pl.BlockSpec((288, WIDE), lambda i: (0, 0), pipeline_mode=pl.Buffered(1))
        ]
        * 4,
        scratch_shapes=[
            pltpu.VMEM((ROWS, WIDE), BF16),
            pltpu.VMEM((8, 16, 256), BF16),
            pltpu.VMEM((ROWS, WIDE), BF16),
            pltpu.VMEM((8, 16, 256), BF16),
            pltpu.VMEM((ROWS, WIDE), BF16),
            pltpu.VMEM((3, 512, WIDE), F32),
            pltpu.VMEM((512, ROWS), BF16),
            pltpu.VMEM((WIDE, WIDE), F32),
            pltpu.SemaphoreType.DMA((4, 8)),
            pltpu.SemaphoreType.DMA((2, 8)),
        ],
        compiler_params=pltpu.CompilerParams(
            dimension_semantics=("arbitrary",), vmem_limit_bytes=VMEM_BYTES
        ),
        cost_estimate=pl.CostEstimate(
            flops=4 * 7 * 512 * 512 * WIDE + 2 * ROWS * WIDE * WIDE,
            bytes_accessed=25_000_000,
            transcendentals=7 * 512 * 512,
        ),
        name="late_pairs",
    )(at, knobs, early, *own, *over, *own_rows)


def place_kernel(*refs):
    pieces, outs = refs[:8], refs[8:10]
    wide, sems = refs[10:]
    core, at_x, at_y = (lax.axis_index(axis) for axis in ("c", "x", "y"))

    def stores(i):
        mine = i < 4
        head = core if mine else 1 - core
        at = jnp.where(head == 0, at_x, at_y)
        row = pl.multiple_of(lax.rem(at + 4 - (0, 1, 3, 2)[i % 4], 4) * 288, 288)
        for h in range(2):
            copy = pltpu.make_async_copy(wide.at[i], outs[h].at[pl.ds(row, 288), :], sems.at[i])
            yield head == h, copy

    for i in (0, 4, 1, 5, 2, 6, 3, 7):
        wide[i] = pieces[i][...].astype(F32)
        for here, copy in stores(i):
            pl.when(here)(copy.start)
    for i in range(8):
        for here, copy in stores(i):
            pl.when(here)(copy.wait)


def place(pieces):
    anywhere = pl.BlockSpec(memory_space=pl.ANY)
    return pl.pallas_call(
        place_kernel,
        out_shape=[jax.ShapeDtypeStruct((WIDE, WIDE), F32)] * 2,
        in_specs=[pl.BlockSpec(memory_space=pltpu.VMEM)] * 8,
        out_specs=[anywhere] * 2,
        scratch_shapes=[pltpu.VMEM((8, 288, WIDE), F32), pltpu.SemaphoreType.DMA((8,))],
        compiler_params=pltpu.CompilerParams(vmem_limit_bytes=16 * 1024 * 1024),
        name="place",
    )(*pieces)


def added(total, parts):
    for part in parts:
        total = total + part.astype(F32)
    return total


def scattered(value, by_route, mine):
    rows = value.shape[0] // 4
    total = lax.dynamic_slice_in_dim(value, mine * rows, rows, 0)
    parts = []
    for by in (1, 3, 2):
        part = lax.dynamic_slice_in_dim(value, lax.rem(mine + by, 4) * rows, rows, 0)
        parts.append(send(part, by_route(by)))
    return added(total, parts)


def local(image_embed, text_embed, image_head, text_head, pair_ids, logit_scale, logit_bias):
    first = lax.axis_index("c") == 0
    scale = logit_scale[0]
    half = scale * (0.5 / math.sqrt(16384))
    knobs = jnp.stack([scale * 0.5, logit_bias[0] * 0.5, half])

    ids_row = jnp.concatenate(
        [(pair_ids // 64).astype(BF16), (pair_ids % 64).astype(BF16), jnp.zeros((896,), BF16)]
    )[None]
    ids_rows = jnp.concatenate([ids_row, jnp.zeros((15, WIDE), BF16)], axis=0)
    mine = jnp.concatenate([jnp.where(first, image_embed, text_embed), ids_rows], axis=0)
    theirs = jnp.concatenate([jnp.where(first, text_embed, image_embed), ids_rows], axis=0)
    heads = (jnp.where(first, image_head, text_head), jnp.where(first, text_head, image_head))

    got = [send(mine, z_pair(0)), send(theirs, z_pair(1))]
    mine, theirs = [
        jnp.concatenate(
            [block[:128], other[:128], block[128:129], other[128:129], block[130:]], axis=0
        )
        for block, other in zip((mine, theirs), got)
    ]
    blocks = [(mine, theirs)]
    for by in (1, 3, 2):
        blocks.append((send(mine, ring(by, 0)), send(theirs, ring(by, 1))))
    own, over, own_rows = [], [], []

    def take(turn):
        message, rows = project(*blocks[turn], heads)
        own.append(message)
        over.append(send(message, other_core))
        own_rows.append(rows)

    for turn in range(3):
        take(turn)
    early = early_pairs(knobs, own, over)
    blocks[3], early = lax.optimization_barrier((blocks[3], early))
    take(3)

    at_x = lax.axis_index("x")
    at_y = lax.axis_index("y")
    at_first = jnp.where(first, at_x, at_y)
    at_second = jnp.where(first, at_y, at_x)
    part, *away = late_pairs(at_first[None], knobs, early, own, over, own_rows)
    part = added(part, [send(piece, ring(by, 0)) for by, piece in zip((1, 3, 2), away)])
    part = scattered(part, lambda by: ring(by, 1), at_second)
    moved = [send(part, z_ring(by)) for by in (1, 3, 2)]
    at_z = lax.axis_index("zh") * 2 + lax.axis_index("zl")
    stack = jnp.zeros((4,) + part.shape, F32)
    for by, piece in zip((0, 1, 3, 2), [part] + moved):
        stack = lax.dynamic_update_slice_in_dim(stack, piece[None], lax.rem(at_z + 4 - by, 4), 0)
    part = ((stack[0] + stack[1]) + (stack[2] + stack[3])).astype(BF16)

    quarter = jnp.zeros((288, WIDE), BF16)
    for by in (0, 1, 3, 2):
        piece = part if by == 0 else send(part, ring(by, 1))
        quarter = lax.dynamic_update_slice_in_dim(
            quarter, piece, lax.rem(at_second + 4 - by, 4) * 72, 0
        )
    pieces = [quarter] + [send(quarter, ring(by, 0)) for by in (1, 3, 2)]
    pieces = pieces + [send(piece, other_core) for piece in pieces]
    return tuple(place(pieces))


def solution(mesh):
    split = Mesh(mesh.devices.reshape(SIZES), AXES)
    every = P(AXES)
    return jax.shard_map(
        local,
        mesh=split,
        in_specs=(every, every, P(), P(), every, P(), P()),
        out_specs=(P(), P()),
        check_vma=False,
    )
```

```python
import functools
import math

import jax
import jax.numpy as jnp
from jax import lax
from jax.experimental import pallas as pl
from jax.experimental.pallas import tpu as pltpu
from jax.sharding import Mesh, PartitionSpec as P

AXES = ("zl", "y", "c", "x", "zh")
SIZES = (2, 4, 2, 4, 2)
BF16 = jnp.bfloat16
F32 = jnp.float32
WIDE = 1152
ROWS = 2048
VMEM_BYTES = 60 * 1024 * 1024


def routes(move):
    pairs = []
    index = 0
    for zl in range(2):
        for y in range(4):
            for c in range(2):
                for x in range(4):
                    for zh in range(2):
                        tzl, ty, tc, tx, tzh = move(zl, y, c, x, zh)
                        pairs.append((index, (((tzl * 4 + ty) * 2 + tc) * 4 + tx) * 2 + tzh))
                        index += 1
    return pairs


def send(value, move):
    return lax.ppermute(value, AXES, routes(move))


def other_core(zl, y, c, x, zh):
    return (zl, y, 1 - c, x, zh)


def z_pair(swap):
    def move(zl, y, c, x, zh):
        return (1 - zl, y, c, x, zh if (c ^ swap) == 0 else 1 - zh)

    return move


def ring(by, swap):
    def move(zl, y, c, x, zh):
        if (c ^ swap) == 0:
            return (zl, y, c, (x + by) % 4, zh)
        return (zl, (y + by) % 4, c, x, zh)

    return move


def z_ring(by):
    def move(zl, y, c, x, zh):
        z = (zh * 2 + zl + by) % 4
        return (z % 2, y, c, x, z // 2)

    return move


def eye_256():
    return lax.broadcasted_iota(jnp.int32, (256, 256), 0) == lax.broadcasted_iota(
        jnp.int32, (256, 256), 1
    )


def as_column(row):
    return jnp.sum(jnp.where(eye_256(), row, 0.0), axis=1, keepdims=True)


def id_row(coded):
    coded = coded.astype(F32)
    parts = [coded[i : i + 1, :128] * 64.0 + coded[i : i + 1, 128:256] for i in (0, 1)]
    return jnp.concatenate(parts, axis=1)


def project_kernel(near, far, head_near, head_far, message, rows_near):
    sides = ((near, head_near, rows_near, 0, 0), (far, head_far, message, 544, 272))
    for block, head, rows, at, to in sides:
        if rows.shape[0] > at:
            rows[at : at + 256, :] = block[:256, :]
        projected = jnp.dot(block[:256, :], head[...], preferred_element_type=F32)
        inverse = lax.rsqrt(jnp.sum(projected * projected, axis=1, keepdims=True) + 1e-06)
        message[to : to + 256, :] = (projected * inverse).astype(BF16)
        message[to + 256 : to + 272, :] = block[256:272, :]
        rest = jnp.sum(jnp.where(eye_256(), inverse, 0.0), axis=0, keepdims=True)
        lines = lax.broadcasted_iota(jnp.int32, (16, 256), 0)
        coded = block[256:272, :256].astype(F32)
        for line in (2, 3, 4):
            part = rest.astype(BF16).astype(F32)
            coded = jnp.where(lines == line, part, coded)
            rest = rest - part
        message[to + 256 : to + 272, :256] = coded.astype(BF16)


def project(near, far, heads, message_rows):
    whole = pl.BlockSpec(memory_space=pltpu.VMEM)
    return pl.pallas_call(
        project_kernel,
        out_shape=[
            jax.ShapeDtypeStruct((message_rows, WIDE), BF16),
            jax.ShapeDtypeStruct((256, WIDE), BF16),
        ],
        in_specs=[whole] * 4,
        out_specs=[whole] * 2,
        compiler_params=pltpu.CompilerParams(vmem_limit_bytes=28 * 1024 * 1024),
        cost_estimate=pl.CostEstimate(
            flops=2 * 512 * WIDE * WIDE, bytes_accessed=8_000_000, transcendentals=0
        ),
        name="project",
    )(near, far, *heads)


def unit_loads(sources, units, ids, unit_sems, id_sems):
    loads = []
    for i, (source, start) in enumerate(sources):
        rows = source.at[pl.ds(start, 256), :]
        coded = source.at[pl.ds(start + 256, 16), pl.ds(0, 256)]
        loads.append(
            (
                pltpu.make_async_copy(rows, units.at[pl.ds(i * 256, 256), :], unit_sems.at[i]),
                pltpu.make_async_copy(coded, ids.at[i], id_sems.at[i]),
            )
        )
    return loads


def pair_coefs(knob_ref, near, column, unit, ids, coef, parts):
    half_scale, half_bias, half = knob_ref[0], knob_ref[1], knob_ref[2]
    for part in parts:
        cosine = lax.dot_general(
            near,
            unit[part * 256 : part * 256 + 256, :],
            (((1,), (1,)), ((), ())),
            preferred_element_type=F32,
        )
        base = jnp.where(column == id_row(ids[part]), -half, half)
        value = jnp.tanh(cosine * half_scale + half_bias) * half + base
        coef[:, pl.ds(part * 256, 256)] = value.astype(BF16)


def chunk_column(ids, step):
    return jnp.concatenate([as_column(id_row(ids[2 * step + i])) for i in range(2)], axis=0)


def chunk_inverse(ids, step):
    parts = []
    for i in range(2):
        coded = ids[2 * step + i].astype(F32)
        parts.append(as_column(coded[2:3] + coded[3:4] + coded[4:5]))
    return jnp.concatenate(parts, axis=0)


def unit_sources(own, over):
    near, far = [], []
    for mine, theirs in zip(own, over):
        near += [(mine, 0), (theirs, 272)]
        far += [(mine, 272), (theirs, 0)]
    return near, far


def early_kernel(knob_ref, *refs):
    near_sources, far_sources = unit_sources(refs[:3], refs[3:6])
    grad, near, near_ids, far, far_ids, coef, sems = refs[6:]
    step = pl.program_id(0)
    near_loads = unit_loads(near_sources, near, near_ids, sems.at[0], sems.at[1])
    far_loads = unit_loads(far_sources, far, far_ids, sems.at[2], sems.at[3])

    @pl.when(step == 0)
    def _():
        for pair in far_loads + near_loads:
            for load in pair:
                load.start()
        for pair in far_loads:
            for load in pair:
                load.wait()

    for i, pair in enumerate(near_loads):

        @pl.when(step == i // 2)
        def _(pair=pair):
            for load in pair:
                load.wait()

    rows = near[pl.ds(pl.multiple_of(step * 512, 512), 512), :]
    pair_coefs(knob_ref, rows, chunk_column(near_ids, step), far, far_ids, coef, range(6))
    grad[...] = jnp.dot(coef[...], far[...], preferred_element_type=F32)


def early_pairs(knobs, own, over):
    return pl.pallas_call(
        early_kernel,
        grid=(3,),
        out_shape=jax.ShapeDtypeStruct((1536, WIDE), F32),
        in_specs=[pl.BlockSpec(memory_space=pltpu.SMEM)]
        + [pl.BlockSpec(memory_space=pl.ANY)] * 6,
        out_specs=pl.BlockSpec((512, WIDE), lambda i: (i, 0)),
        scratch_shapes=[
            pltpu.VMEM((1536, WIDE), BF16),
            pltpu.VMEM((6, 16, 256), BF16),
            pltpu.VMEM((1536, WIDE), BF16),
            pltpu.VMEM((6, 16, 256), BF16),
            pltpu.VMEM((512, 1536), BF16),
            pltpu.SemaphoreType.DMA((4, 6)),
        ],
        compiler_params=pltpu.CompilerParams(
            dimension_semantics=("arbitrary",), vmem_limit_bytes=40 * 1024 * 1024
        ),
        cost_estimate=pl.CostEstimate(
            flops=4 * 1536 * 1536 * WIDE, bytes_accessed=14_000_000, transcendentals=1536 * 1536
        ),
        name="early_pairs",
    )(knobs, *own, *over)


def late_kernel(at_ref, knob_ref, early, *refs):
    own, over, own_rows, outs = refs[:4], refs[4:8], refs[8:12], refs[13:17]
    over_rows = [block.at[pl.ds(544, 256), :] for block in over[:3]]
    over_rows.append(refs[12].at[pl.ds(0, 256), :])
    near, near_ids, far, far_ids, rows, grad, coef, total, sems, more_sems = refs[17:]
    near_sources, far_sources = unit_sources(own, over)
    step = pl.program_id(0)
    near_loads = unit_loads(near_sources, near, near_ids, sems.at[0], sems.at[1])
    far_loads = unit_loads(far_sources, far, far_ids, sems.at[2], sems.at[3])
    for i in range(8):
        source = over_rows[i // 2] if i % 2 else own_rows[i // 2]
        near_loads[i] += (
            pltpu.make_async_copy(source, rows.at[pl.ds(i * 256, 256), :], more_sems.at[0, i]),
        )
    for i in range(3):
        near_loads[2 * i] += (
            pltpu.make_async_copy(
                early.at[pl.ds(512 * i, 512), :], grad.at[i], more_sems.at[1, i]
            ),
        )

    @pl.when(step == 0)
    def _():
        for pair in far_loads[6:] + near_loads[:2]:
            for load in pair:
                load.start()
        for pair in far_loads[6:]:
            for load in pair:
                load.wait()
        total[...] = jnp.zeros_like(total)

    for i, pair in enumerate(near_loads):

        @pl.when(step == i // 2)
        def _(pair=pair):
            for load in pair:
                load.wait()

    @pl.when(step == 0)
    def _():
        for pair in near_loads[2:] + far_loads[:6]:
            for load in pair:
                load.start()

    at = pl.ds(pl.multiple_of(step * 512, 512), 512)
    column = chunk_column(near_ids, step)
    inverse = chunk_inverse(near_ids, step)

    def finish(gradient):
        direction = near[at, :].astype(F32)
        radial = jnp.sum(gradient * direction, axis=1, keepdims=True)
        back = ((gradient - radial * direction) * inverse).astype(BF16)
        total[...] += lax.dot_general(
            rows[at, :], back, (((0,), (0,)), ((), ())), preferred_element_type=F32
        )

    @pl.when(step < 3)
    def _():
        pair_coefs(knob_ref, near[at, :], column, far, far_ids, coef, (6, 7))
        more = jnp.dot(coef[:, 1536:], far[1536:, :], preferred_element_type=F32)
        finish(grad[step] + more)

    @pl.when(step == 3)
    def _():
        for pair in far_loads[:6]:
            for load in pair:
                load.wait()
        pair_coefs(knob_ref, near[at, :], column, far, far_ids, coef, range(8))
        finish(jnp.dot(coef[...], far[...], preferred_element_type=F32))
        for by, out in zip((0, 1, 3, 2), outs):
            place = pl.multiple_of(lax.rem(at_ref[0] + by, 4) * 288, 288)
            out[...] = total[pl.ds(place, 288), :].astype(out.dtype)


def late_pairs(at, knobs, early, own, over, own_rows, last_rows):
    smem = pl.BlockSpec(memory_space=pltpu.SMEM)
    return pl.pallas_call(
        late_kernel,
        grid=(4,),
        out_shape=[jax.ShapeDtypeStruct((288, WIDE), kind) for kind in (F32, BF16, BF16, BF16)],
        in_specs=[smem, smem] + [pl.BlockSpec(memory_space=pl.ANY)] * 14,
        out_specs=[
            pl.BlockSpec((288, WIDE), lambda i: (0, 0), pipeline_mode=pl.Buffered(1))
        ]
        * 4,
        scratch_shapes=[
            pltpu.VMEM((ROWS, WIDE), BF16),
            pltpu.VMEM((8, 16, 256), BF16),
            pltpu.VMEM((ROWS, WIDE), BF16),
            pltpu.VMEM((8, 16, 256), BF16),
            pltpu.VMEM((ROWS, WIDE), BF16),
            pltpu.VMEM((3, 512, WIDE), F32),
            pltpu.VMEM((512, ROWS), BF16),
            pltpu.VMEM((WIDE, WIDE), F32),
            pltpu.SemaphoreType.DMA((4, 8)),
            pltpu.SemaphoreType.DMA((2, 8)),
        ],
        compiler_params=pltpu.CompilerParams(
            dimension_semantics=("arbitrary",), vmem_limit_bytes=VMEM_BYTES
        ),
        cost_estimate=pl.CostEstimate(
            flops=4 * 7 * 512 * 512 * WIDE + 2 * ROWS * WIDE * WIDE,
            bytes_accessed=25_000_000,
            transcendentals=7 * 512 * 512,
        ),
        name="late_pairs",
    )(at, knobs, early, *own, *over, *own_rows, last_rows)


def place_kernel(*refs):
    pieces, outs = refs[:8], refs[8:10]
    wide, sems = refs[10:]
    core, at_x, at_y = (lax.axis_index(axis) for axis in ("c", "x", "y"))

    def stores(i):
        mine = i < 4
        head = core if mine else 1 - core
        at = jnp.where(head == 0, at_x, at_y)
        row = pl.multiple_of(lax.rem(at + 4 - (0, 1, 3, 2)[i % 4], 4) * 288, 288)
        for h in range(2):
            copy = pltpu.make_async_copy(wide.at[i], outs[h].at[pl.ds(row, 288), :], sems.at[i])
            yield head == h, copy

    for i in (0, 4, 1, 5, 2, 6, 3, 7):
        wide[i] = pieces[i][...].astype(F32)
        for here, copy in stores(i):
            pl.when(here)(copy.start)
    for i in range(8):
        for here, copy in stores(i):
            pl.when(here)(copy.wait)


def place(pieces):
    anywhere = pl.BlockSpec(memory_space=pl.ANY)
    return pl.pallas_call(
        place_kernel,
        out_shape=[jax.ShapeDtypeStruct((WIDE, WIDE), F32)] * 2,
        in_specs=[pl.BlockSpec(memory_space=pltpu.VMEM)] * 8,
        out_specs=[anywhere] * 2,
        scratch_shapes=[pltpu.VMEM((8, 288, WIDE), F32), pltpu.SemaphoreType.DMA((8,))],
        compiler_params=pltpu.CompilerParams(vmem_limit_bytes=16 * 1024 * 1024),
        name="place",
    )(*pieces)


def added(total, parts):
    for part in parts:
        total = total + part.astype(F32)
    return total


def scattered(value, by_route, mine):
    rows = value.shape[0] // 4
    total = lax.dynamic_slice_in_dim(value, mine * rows, rows, 0)
    parts = []
    for by in (1, 3, 2):
        part = lax.dynamic_slice_in_dim(value, lax.rem(mine + by, 4) * rows, rows, 0)
        parts.append(send(part, by_route(by)))
    return added(total, parts)


def local(image_embed, text_embed, image_head, text_head, pair_ids, logit_scale, logit_bias):
    first = lax.axis_index("c") == 0
    scale = logit_scale[0]
    half = scale * (0.5 / math.sqrt(16384))
    knobs = jnp.stack([scale * 0.5, logit_bias[0] * 0.5, half])

    ids_row = jnp.concatenate(
        [(pair_ids // 64).astype(BF16), (pair_ids % 64).astype(BF16), jnp.zeros((896,), BF16)]
    )[None]
    ids_rows = jnp.concatenate([ids_row, jnp.zeros((15, WIDE), BF16)], axis=0)
    mine = jnp.concatenate([jnp.where(first, image_embed, text_embed), ids_rows], axis=0)
    theirs = jnp.concatenate([jnp.where(first, text_embed, image_embed), ids_rows], axis=0)
    heads = (jnp.where(first, image_head, text_head), jnp.where(first, text_head, image_head))

    got = [send(mine, z_pair(0)), send(theirs, z_pair(1))]
    mine, theirs = [
        jnp.concatenate(
            [block[:128], other[:128], block[128:129], other[128:129], block[130:]], axis=0
        )
        for block, other in zip((mine, theirs), got)
    ]
    blocks = [(mine, theirs)]
    for by in (1, 3, 2):
        blocks.append((send(mine, ring(by, 0)), send(theirs, ring(by, 1))))
    own, over, own_rows = [], [], []

    def take(turn):
        message, rows = project(*blocks[turn], heads, 800 if turn < 3 else 544)
        own.append(message)
        over.append(send(message, other_core))
        own_rows.append(rows)

    for turn in range(3):
        take(turn)
    early = early_pairs(knobs, own, over)
    blocks[3], early = lax.optimization_barrier((blocks[3], early))
    last_rows = send(blocks[3][1], other_core)
    take(3)

    at_x = lax.axis_index("x")
    at_y = lax.axis_index("y")
    at_first = jnp.where(first, at_x, at_y)
    at_second = jnp.where(first, at_y, at_x)
    part, *away = late_pairs(at_first[None], knobs, early, own, over, own_rows, last_rows)
    part = added(part, [send(piece, ring(by, 0)) for by, piece in zip((1, 3, 2), away)])
    part = scattered(part, lambda by: ring(by, 1), at_second)
    moved = [send(part, z_ring(by)) for by in (1, 3, 2)]
    at_z = lax.axis_index("zh") * 2 + lax.axis_index("zl")
    stack = jnp.zeros((4,) + part.shape, F32)
    for by, piece in zip((0, 1, 3, 2), [part] + moved):
        stack = lax.dynamic_update_slice_in_dim(stack, piece[None], lax.rem(at_z + 4 - by, 4), 0)
    part = ((stack[0] + stack[1]) + (stack[2] + stack[3])).astype(BF16)

    quarter = jnp.zeros((288, WIDE), BF16)
    for by in (0, 1, 3, 2):
        piece = part if by == 0 else send(part, ring(by, 1))
        quarter = lax.dynamic_update_slice_in_dim(
            quarter, piece, lax.rem(at_second + 4 - by, 4) * 72, 0
        )
    pieces = [quarter] + [send(quarter, ring(by, 0)) for by in (1, 3, 2)]
    pieces = pieces + [send(piece, other_core) for piece in pieces]
    return tuple(place(pieces))


def solution(mesh):
    split = Mesh(mesh.devices.reshape(SIZES), AXES)
    every = P(AXES)
    return jax.shard_map(
        local,
        mesh=split,
        in_specs=(every, every, P(), P(), every, P(), P()),
        out_specs=(P(), P()),
        check_vma=False,
    )
```
